32 devices in a mesh: hash: 16 (over z, x, core), tm: 2 (over y).
Axes of the slice: x: 2, y: 2, z: 4, core: 2. Of those that a mesh axis runs over, the one named last changes fastest.
Arguments:
- transactions: float32 [32768, 256], P(('hash', 'tm')), may hold values from -6 to 6
- tx_product: int32 [32768], P(('hash', 'tm')), may hold values from 0 to 255
- tx_count: int32 [512], P(('hash', 'tm')), may hold values from 16 to 64, as said below
- products: float32 [4096, 256], P(('hash', 'tm')), may hold values from -6 to 6
- customers: float32 [8192, 256], P(('hash', 'tm')), may hold values from -6 to 6
- send_rows: int32 [8192], P(('hash', 'tm')), may hold values from 0 to 127
- send_count: int32 [512], P(('hash', 'tm')), may hold values from 0 to 16, as said below
- recv_customer: int32 [8192], P(('hash', 'tm')), may hold values from 0 to 255
- w_msg: float32 [256, 256], replicated, may hold values from -0.375 to 0.375
- w_prod_self: float32 [256, 256], replicated, may hold values from -0.375 to 0.375
- w_prod_agg: float32 [256, 256], replicated, may hold values from -0.375 to 0.375
- w_cust_self: float32 [256, 256], replicated, may hold values from -0.375 to 0.375
- w_cust_prod: float32 [256, 256], replicated, may hold values from -0.375 to 0.375
Outputs:
- new_products: float32 [4096, 256], P(('hash', 'tm'))
- new_customers: float32 [8192, 256], P(('hash', 'tm'))
The draws below stay inside these ranges and needn't reach their ends.
Inputs may be any that keep to these rules, and one draw needn't show every extreme that they name: `tx_count`: each device has at least one product owner for which all 64 slots are used; which one is drawn. `send_count`: uneven counts; each device has at least one customer owner for which all 16 slots are used.
All inputs are finite; a program needn't handle non-finite values.
Results may differ from the reference program's by a relative error of at most 0.000055.
Values sent between devices are 32-bit elements; how exact they have to be, the bound alone decides.
No kernel may reach another device: no remote copies, remote signals or barrier semaphores. Data moves between devices by JAX's collectives and lax.ppermute only.
A program may use at most 64 MiB of HBM per device.

```python
import jax
import jax.numpy as jnp
from jax import lax

D = 256
CAP = 64
P_DEV = 128
C_DEV = 256
SEND_CAP = 16
PH = 256
PROD = 4096
CUST = 8192
TXS = 32768
SENDS = 8192
N_HASH = 16
N_TM = 2


def draw_tx_count(key, part):
    key = jax.random.fold_in(key, 11)
    first, second = jax.random.split(key)
    devices = N_HASH * N_TM
    lowest = max(1, CAP // 4)
    base = jax.random.randint(first, (devices, N_HASH), lowest, CAP + 1)
    chosen = jax.random.randint(second, (devices, 1), 0, N_HASH)
    column = jnp.arange(N_HASH, dtype=jnp.int32)[None, :]
    return jnp.where(column == chosen, CAP, base).reshape(-1).astype(jnp.int32)


def draw_send_count(key, part):
    key = jax.random.fold_in(key, 23)
    first, second, third = jax.random.split(key, 3)
    devices = N_HASH * N_TM
    left = jax.random.randint(first, (devices, N_HASH), 0, SEND_CAP + 1)
    right = jax.random.randint(second, (devices, N_HASH), 0, SEND_CAP + 1)
    base = jnp.minimum(left, right)
    chosen = jax.random.randint(third, (devices, 1), 0, N_HASH)
    column = jnp.arange(N_HASH, dtype=jnp.int32)[None, :]
    return jnp.where(column == chosen, SEND_CAP, base).reshape(-1).astype(jnp.int32)


def place_ends(drawn, own_key, least, high):
    spot = [jax.random.randint(jax.random.fold_in(own_key, axis), (), 0, length) for axis, length in enumerate(drawn.shape)]
    main_axis = drawn.shape.index(max(drawn.shape))
    next_to = spot[:main_axis] + [(spot[main_axis] + 1) % drawn.shape[main_axis]] + spot[main_axis + 1:]
    return drawn.at[tuple(spot)].set(least).at[tuple(next_to)].set(high)


def level_of(stream_key, extent, pieces, smallest, top_value):
    loudness = 1.0
    for axis_at, shards_of in pieces:
        draws = jax.random.uniform(jax.random.fold_in(jax.random.fold_in(stream_key, 6), axis_at), (shards_of,), jnp.float32, smallest / len(pieces), top_value / len(pieces))
        loudness = loudness * jnp.repeat(jnp.exp(draws), extent[axis_at] // shards_of).reshape((-1,) + (1,) * (len(extent) - 1 - axis_at))
    return loudness


def noise(stream_key, extent, spread, bound, shards=(), held_as=jnp.bfloat16):
    level = level_of(stream_key, extent, shards, -0.22, 0.18) if shards else 1.0
    result = jax.random.normal(stream_key, extent, jnp.float32) * spread * level
    return jnp.minimum(jnp.maximum(result, -bound), bound).astype(held_as)


def setup_inputs(seed: int = 0) -> dict:
    keys = jax.random.split(jax.random.key(seed), 14)
    transactions = noise(keys[0], (TXS, D), 1.0, 6.0, ((0, 32),), jnp.float32)
    tx_product = place_ends(jax.random.randint(keys[1], (TXS,), 0, PH), jax.random.fold_in(keys[1], 1), 0, PH - 1).astype(jnp.int32)
    tx_count = draw_tx_count(jax.random.fold_in(keys[13], 71), 0)
    products = noise(keys[3], (PROD, D), 1.0, 6.0, ((0, 32),), jnp.float32)
    customers = noise(keys[4], (CUST, D), 1.0, 6.0, ((0, 32),), jnp.float32)
    send_rows = place_ends(jax.random.randint(keys[5], (SENDS,), 0, P_DEV), jax.random.fold_in(keys[5], 1), 0, P_DEV - 1).astype(jnp.int32)
    send_count = draw_send_count(jax.random.fold_in(keys[13], 71), 0)
    recv_customer = place_ends(jax.random.randint(keys[7], (SENDS,), 0, C_DEV), jax.random.fold_in(keys[7], 1), 0, C_DEV - 1).astype(jnp.int32)
    w_msg = noise(keys[8], (D, D), D ** -0.5, 0.375, (), jnp.float32)
    w_prod_self = noise(keys[9], (D, D), D ** -0.5, 0.375, (), jnp.float32)
    w_prod_agg = noise(keys[10], (D, D), D ** -0.5, 0.375, (), jnp.float32)
    w_cust_self = noise(keys[11], (D, D), D ** -0.5, 0.375, (), jnp.float32)
    w_cust_prod = noise(keys[12], (D, D), D ** -0.5, 0.375, (), jnp.float32)
    return {"transactions": transactions, "tx_product": tx_product, "tx_count": tx_count, "products": products, "customers": customers, "send_rows": send_rows, "send_count": send_count, "recv_customer": recv_customer, "w_msg": w_msg, "w_prod_self": w_prod_self, "w_prod_agg": w_prod_agg, "w_cust_self": w_cust_self, "w_cust_prod": w_cust_prod}


highest = lax.Precision.HIGHEST


def update(table, other, w_self, w_other):
    inner = jnp.dot(table, w_self, precision=highest) + jnp.dot(other, w_other, precision=highest)
    return table + jax.nn.relu(inner)


def reference(transactions, tx_product, tx_count, products, customers, send_rows, send_count, recv_customer, w_msg, w_prod_self, w_prod_agg, w_cust_self, w_cust_prod):
    owned = P_DEV * N_TM
    message = jax.nn.relu(jnp.dot(transactions, w_msg, precision=highest))
    index = jnp.arange(transactions.shape[0], dtype=jnp.int32)
    device = index // (N_HASH * CAP)
    bucket = (index // CAP) % N_HASH
    slot = index % CAP
    used = slot < tx_count[device * N_HASH + bucket]
    target = (bucket * owned + tx_product).astype(jnp.int32)
    message = jnp.where(used[:, None], message, jnp.zeros_like(message))
    aggregate = jax.ops.segment_sum(message, target, num_segments=products.shape[0])
    new_products = update(products, aggregate, w_prod_self, w_prod_agg)
    place = jnp.arange(recv_customer.shape[0], dtype=jnp.int32)
    receiver = place // (N_HASH * SEND_CAP)
    source_owner = (place // SEND_CAP) % N_HASH
    slot_two = place % SEND_CAP
    own_hash = receiver // N_TM
    own_time = receiver % N_TM
    source = source_owner * N_TM + own_time
    list_pos = ((source * N_HASH + own_hash) * SEND_CAP + slot_two).astype(jnp.int32)
    row = source * P_DEV + send_rows[list_pos]
    live = slot_two < send_count[source * N_HASH + own_hash]
    carried = new_products[row.astype(jnp.int32)]
    carried = jnp.where(live[:, None], carried, jnp.zeros_like(carried))
    customer_id = (receiver * C_DEV + recv_customer).astype(jnp.int32)
    bought = jax.ops.segment_sum(carried, customer_id, num_segments=customers.shape[0])
    new_customers = update(customers, bought, w_cust_self, w_cust_prod)
    return new_products, new_customers
```

```python
import jax
import jax.numpy as jnp
from jax import lax
from jax.sharding import PartitionSpec as P

high = lax.Precision.HIGH


def swap_bit(blocks, axis, bit, mask, peers):
    keep = lax.dynamic_index_in_dim(blocks, bit, axis, keepdims=True)
    send = lax.dynamic_index_in_dim(blocks, 1 - bit, axis, keepdims=True)
    got = lax.ppermute(send, "hash", [(i, i ^ mask) for i in range(peers)])
    low = jnp.where(bit == 0, keep, got)
    top = jnp.where(bit == 0, got, keep)
    return jnp.concatenate([low, top], axis)


def exchange_ids(ids):
    peers, slots = ids.shape
    if peers != 16:
        return lax.all_to_all(ids, "hash", split_axis=0, concat_axis=0, tiled=True)
    me = lax.axis_index("hash")
    blocks = ids.reshape(4, 2, 2, slots)
    blocks = swap_bit(blocks, 2, me & 1, 1, peers)
    blocks = swap_bit(blocks, 1, (me >> 1) & 1, 2, peers)
    far = me >> 2
    got = [lax.dynamic_index_in_dim(blocks, far, 0, keepdims=False)]
    for k in (1, 2, 3):
        send = lax.dynamic_index_in_dim(blocks, far ^ k, 0, keepdims=False)
        got.append(lax.ppermute(send, "hash", [(i, i ^ (4 * k)) for i in range(peers)]))
    stacked = jnp.stack(got)
    order = [lax.dynamic_index_in_dim(stacked, far ^ k, 0, keepdims=True) for k in range(4)]
    return jnp.concatenate(order, 0).reshape(peers, slots)


def local(
    transactions,
    tx_product,
    tx_count,
    products,
    customers,
    send_rows,
    send_count,
    recv_customer,
    w_msg,
    w_prod_self,
    w_prod_agg,
    w_cust_self,
    w_cust_prod,
):
    peers, pair = lax.axis_size("hash"), lax.axis_size("tm")
    half = lax.axis_index("tm")
    width = transactions.shape[1]
    slots = transactions.shape[0] // peers
    mine = products.shape[0]
    send_slots = send_rows.shape[0] // peers

    slot_index = lax.broadcasted_iota(jnp.int32, (peers, slots), 1)
    ids = jnp.where(slot_index < tx_count[:, None], tx_product.reshape(peers, slots), -1)
    outgoing = jax.nn.relu(jnp.dot(transactions, w_msg, precision=high))
    arrived = lax.all_to_all(
        outgoing.reshape(peers, slots, width), "hash", split_axis=0, concat_axis=0, tiled=True
    ).reshape(-1, width)
    flat_ids = exchange_ids(ids).reshape(-1)

    product_self = jnp.dot(products, w_prod_self, precision=high)
    customer_self = jnp.dot(customers, w_cust_self, precision=high)

    def block_sum(part):
        targets = part * mine + lax.iota(jnp.int32, mine)
        onehot = (flat_ids[None, :] == targets[:, None]).astype(jnp.float32)
        return jnp.dot(onehot, arrived, precision=high)

    if pair == 2:
        other = lax.ppermute(block_sum(1 - half), "tm", [(0, 1), (1, 0)])
        aggregate = block_sum(half) + other
    else:
        parts = lax.map(block_sum, jnp.arange(pair)).reshape(pair * mine, width)
        aggregate = lax.psum_scatter(parts, "tm", scatter_dimension=0, tiled=True)
    inner = product_self + jnp.dot(aggregate, w_prod_agg, precision=high)
    new_products = products + jax.nn.relu(inner)

    send_index = lax.broadcasted_iota(jnp.int32, (peers, send_slots), 1)
    named = jnp.where(send_index < send_count[:, None], send_rows.reshape(peers, send_slots), -1)
    picks = (named.reshape(-1)[:, None] == lax.iota(jnp.int32, mine)[None, :]).astype(jnp.float32)
    listed = jnp.dot(picks, new_products, precision=high).reshape(peers, send_slots, width)
    incoming = lax.all_to_all(listed, "hash", split_axis=0, concat_axis=0, tiled=True)
    customer_rows = lax.iota(jnp.int32, customers.shape[0])
    incidence = (recv_customer[None, :] == customer_rows[:, None]).astype(jnp.float32)
    bought = jnp.dot(incidence, incoming.reshape(-1, width), precision=high)
    inner = customer_self + jnp.dot(bought, w_cust_prod, precision=high)
    return new_products, customers + jax.nn.relu(inner)


def solution(mesh):
    rows, flat = P(("hash", "tm"), None), P(("hash", "tm"))
    placed = (rows, flat, flat, rows, rows, flat, flat, flat, P(), P(), P(), P(), P())
    return jax.shard_map(local, mesh=mesh, in_specs=placed, out_specs=(rows, rows), check_vma=False)
```

```python
import jax
import jax.numpy as jnp
from jax import lax
from jax.experimental import pallas as pl
from jax.experimental.pallas import tpu as pltpu
from jax.sharding import PartitionSpec as P

high = lax.Precision.HIGH
f32, bf16 = jnp.float32, jnp.bfloat16


def split(x):
    top = x.astype(bf16)
    return top, (x - top.astype(f32)).astype(bf16)


def split_outside(x):
    top = lax.reduce_precision(x, 8, 7)
    return top.astype(bf16), (x - top).astype(bf16)


def mm(a, b):
    return jnp.dot(a, b, preferred_element_type=f32)


def dot3(x, w_top, w_low):
    top, low = split(x)
    return mm(top, w_top) + (mm(low, w_top) + mm(top, w_low))


def dot2(picks, x):
    top, low = split(x)
    return mm(picks, top) + mm(picks, low)


def call(kernel, out, ins):
    vmem = pl.BlockSpec(memory_space=pltpu.VMEM)
    return pl.pallas_call(
        kernel,
        out_shape=[jax.ShapeDtypeStruct(s, f32) for s in out],
        in_specs=[vmem] * len(ins),
        out_specs=[vmem] * len(out),
        compiler_params=pltpu.CompilerParams(vmem_limit_bytes=32 * 1024 * 1024),
    )(*ins)


def message_kernel(x, w, out):
    out[...] = jnp.maximum(dot3(x[...], *split(w[...])), 0.0).reshape(out.shape)


def messages(transactions, w_msg, peers):
    rows, width = transactions.shape
    slots, steps = rows // peers, 4
    return pl.pallas_call(
        message_kernel,
        grid=(steps,),
        out_shape=jax.ShapeDtypeStruct((peers, slots, width), f32),
        in_specs=[
            pl.BlockSpec((rows // steps, width), lambda i: (i, 0)),
            pl.BlockSpec((width, width), lambda i: (0, 0)),
        ],
        out_specs=pl.BlockSpec((peers // steps, slots, width), lambda i: (i, 0, 0)),
        compiler_params=pltpu.CompilerParams(vmem_limit_bytes=32 * 1024 * 1024),
    )(transactions, w_msg)


def sum_kernel(picks, x, out):
    out[...] = dot2(picks[...], x[...])


def update_kernel(kept, got, own, table, w_top, w_low, picks, new, listed):
    fresh = table[...] + jnp.maximum(own[...] + dot3(kept[...] + got[...], w_top[...], w_low[...]), 0.0)
    new[...] = fresh
    listed[...] = dot2(picks[...], fresh).reshape(listed.shape)


def final_kernel(incoming, incidence, own, table, w_top, w_low, new):
    bought = dot2(incidence[...], incoming[...])
    new[...] = table[...] + jnp.maximum(own[...] + dot3(bought, w_top[...], w_low[...]), 0.0)


def swap(x, axis, mask, size):
    return lax.ppermute(x, axis, [(i, i ^ mask) for i in range(size)])


def spread(x):
    return lax.all_to_all(x, "hash", split_axis=0, concat_axis=0, tiled=True)


def pick(x, i, axis=0):
    return lax.dynamic_index_in_dim(x, i, axis, keepdims=True)


def swap_bit(blocks, axis, bit, mask, peers):
    keep = pick(blocks, bit, axis)
    got = swap(pick(blocks, 1 - bit, axis), "hash", mask, peers)
    return jnp.concatenate([jnp.where(bit == 0, keep, got), jnp.where(bit == 0, got, keep)], axis)


def spread_both(outgoing, ids):
    peers, slots = ids.shape
    if peers != 16:
        return spread(outgoing), spread(ids)
    me = lax.axis_index("hash")
    far = me >> 2
    blocks = ids.reshape(4, 2, 2, slots)
    got = [pick(blocks, far)] + [swap(pick(blocks, far ^ k), "hash", 4 * k, peers) for k in (1, 2, 3)]
    outgoing, *got = lax.optimization_barrier((outgoing, *got))
    arrived = spread(outgoing)
    stacked = jnp.concatenate(got, 0)
    blocks = jnp.concatenate([pick(stacked, far ^ k) for k in range(4)], 0)
    blocks = swap_bit(blocks, 2, me & 1, 1, peers)
    blocks = swap_bit(blocks, 1, (me >> 1) & 1, 2, peers)
    return arrived, blocks.reshape(peers, slots)


def local(
    transactions,
    tx_product,
    tx_count,
    products,
    customers,
    send_rows,
    send_count,
    recv_customer,
    w_msg,
    w_prod_self,
    w_prod_agg,
    w_cust_self,
    w_cust_prod,
):
    peers, pair = lax.axis_size("hash"), lax.axis_size("tm")
    half = lax.axis_index("tm")
    width = transactions.shape[1]
    slots = transactions.shape[0] // peers
    mine = products.shape[0]
    send_slots = send_rows.shape[0] // peers

    slot_index = lax.broadcasted_iota(jnp.int32, (peers, slots), 1)
    ids = jnp.where(slot_index < tx_count[:, None], tx_product.reshape(peers, slots), -1)
    arrived, ids = spread_both(messages(transactions, w_msg, peers), ids)
    arrived, ids = arrived.reshape(-1, width), ids.reshape(-1)

    def part_sum(part):
        picks = (ids[None, :] == (part * mine + lax.iota(jnp.int32, mine))[:, None]).astype(bf16)
        return call(sum_kernel, [(mine, width)], (picks, arrived))[0]

    if pair == 2:
        got = swap(part_sum(1 - half), "tm", 1, 2)
        kept = part_sum(half)
    else:
        parts = jnp.concatenate([part_sum(i) for i in range(pair)])
        kept = lax.psum_scatter(parts, "tm", scatter_dimension=0, tiled=True)
        got = jnp.zeros_like(kept)

    product_self = jnp.dot(products, w_prod_self, precision=high)
    customer_self = jnp.dot(customers, w_cust_self, precision=high)
    send_index = lax.broadcasted_iota(jnp.int32, (peers, send_slots), 1)
    named = jnp.where(send_index < send_count[:, None], send_rows.reshape(peers, send_slots), -1).reshape(-1)
    picks = (named[:, None] == lax.iota(jnp.int32, mine)[None, :]).astype(bf16)
    incidence = (recv_customer[None, :] == lax.iota(jnp.int32, customers.shape[0])[:, None]).astype(bf16)

    new_products, listed = call(
        update_kernel,
        [products.shape, (peers, send_slots, width)],
        (kept, got, product_self, products, *split_outside(w_prod_agg), picks),
    )
    incoming = spread(listed).reshape(-1, width)
    (new_customers,) = call(
        final_kernel,
        [customers.shape],
        (incoming, incidence, customer_self, customers, *split_outside(w_cust_prod)),
    )
    return new_products, new_customers


def solution(mesh):
    rows, flat = P(("hash", "tm"), None), P(("hash", "tm"))
    placed = (rows, flat, flat, rows, rows, flat, flat, flat, P(), P(), P(), P(), P())
    return jax.shard_map(local, mesh=mesh, in_specs=placed, out_specs=(rows, rows), check_vma=False)
```

```python
import jax
import jax.numpy as jnp
from jax import lax
from jax.experimental import pallas as pl
from jax.experimental.pallas import tpu as pltpu
from jax.sharding import PartitionSpec as P

high = lax.Precision.HIGH
f32, bf16 = jnp.float32, jnp.bfloat16
LANES = 128
PAD = 8


def split(x):
    top = x.astype(bf16)
    return top, (x - top.astype(f32)).astype(bf16)


def split_outside(x):
    top = lax.reduce_precision(x, 8, 7)
    return top.astype(bf16), (x - top).astype(bf16)


def mm(a, b):
    return jnp.dot(a, b, preferred_element_type=f32)


def dot3(x, w_top, w_low):
    top, low = split(x)
    return mm(top, w_top) + (mm(low, w_top) + mm(top, w_low))


def dot2(picks, x):
    top, low = split(x)
    return mm(picks, top) + mm(picks, low)


def call(kernel, out, ins, smem=()):
    vmem = pl.BlockSpec(memory_space=pltpu.VMEM)
    scalar = pl.BlockSpec(memory_space=pltpu.SMEM)
    return pl.pallas_call(
        kernel,
        out_shape=[jax.ShapeDtypeStruct(s, f32) for s in out],
        in_specs=[scalar] * len(smem) + [vmem] * len(ins),
        out_specs=[vmem] * len(out),
        compiler_params=pltpu.CompilerParams(vmem_limit_bytes=32 * 1024 * 1024),
    )(*smem, *ins)


def lanes():
    return lax.broadcasted_iota(jnp.int32, (1, LANES), 1)


def message_kernel(place, count, tx, ids, w, p0, p1, p2, p3, q0, q1, q2, q3):
    near = place[0] & 3
    w_top, w_low = split(w[...])
    slots = q0.shape[1]
    lane = lanes()
    for m, (first, second) in enumerate(((p0, q0), (p1, q1), (p2, q2), (p3, q3))):
        c = near ^ m
        x = jnp.concatenate([tx[pl.ds(pl.multiple_of((4 * z + c) * slots, slots), slots), :] for z in range(4)], 0)
        y = jnp.maximum(dot3(x, w_top, w_low), 0.0)
        first[:, :slots, :] = y[:, :LANES].reshape(4, slots, LANES)
        second[...] = y[:, LANES:].reshape(4, slots, LANES)
        for z in range(4):
            row = ids[pl.ds(2 * z + (c >> 1), 1), :]
            turned = pltpu.roll(row, slots, 1)
            twice = jnp.where((lane >= slots).astype(jnp.int32) == (c & 1), row, turned)
            twice = jnp.where((lane & (slots - 1)) < count[4 * z + c], twice, -1).astype(f32)
            first[z, slots:, :] = jnp.broadcast_to(twice, (PAD, LANES))


def sums(place, rows, blocks, send, keep):
    mine = send.shape[1]
    slots = LANES // 2
    own = place[1]
    row = lax.broadcasted_iota(jnp.int32, (2 * mine, LANES), 0)
    target = jnp.where(row < mine, row + (1 - own) * mine, row - mine + own * mine).astype(f32)
    for z in range(4):
        picks = jnp.concatenate([(r == target).astype(bf16) for r in rows[z]], 1)
        top, low = split(jnp.concatenate([block[z, :slots, :] for block in blocks], 0))
        total = mm(picks, jnp.concatenate([top, low], 1))
        total = total[:, :LANES] + total[:, LANES:]
        send[z] = total[:mine]
        keep[z] = total[mine:]


def first_sum_kernel(place, r0, r1, r2, r3, send, keep, ids):
    slots = r0.shape[1] - PAD
    lane = lanes()
    rows = []
    for z in range(4):
        one = [block[z, pl.ds(slots, 1), :] for block in (r0, r1, r2, r3)]
        rows.append([jnp.where(lane < slots, one[i], one[i + 1]) for i in (0, 2)])
        for i in range(2):
            ids[pl.ds(2 * z + i, 1), :] = rows[z][i]
    sums(place, rows, (r0, r1, r2, r3), send, keep)


def second_sum_kernel(place, ids, r0, r1, r2, r3, send, keep):
    rows = [[ids[pl.ds(2 * z + i, 1), :] for i in range(2)] for z in range(4)]
    sums(place, rows, (r0, r1, r2, r3), send, keep)


def pair_kernel(place, keep, got, b0, b1, b2, b3):
    far = place[0] >> 2
    for k, out in enumerate((b0, b1, b2, b3)):
        out[...] = keep[far ^ k] + got[far ^ k]


def update_kernel(*refs):
    parts, (own, table, w_top, w_low, picks, new, listed) = refs[:-7], refs[-7:]
    n = len(parts) // 2
    halves = [sum(part[...] for part in side) for side in (parts[:n], parts[n:])]
    gathered = jnp.concatenate(halves, 1)
    fresh = table[...] + jnp.maximum(own[...] + dot3(gathered, w_top[...], w_low[...]), 0.0)
    new[...] = fresh
    listed[...] = dot2(picks[...], fresh).reshape(listed.shape)


def final_kernel(incoming, incidence, own, table, w_top, w_low, new):
    bought = dot2(incidence[...], incoming[...])
    new[...] = table[...] + jnp.maximum(own[...] + dot3(bought, w_top[...], w_low[...]), 0.0)


def swap(x, axis, mask, size):
    return lax.ppermute(x, axis, [(i, i ^ mask) for i in range(size)])


def spread(x):
    return lax.all_to_all(x, "hash", split_axis=0, concat_axis=0, tiled=True)


def gathered_by_permutes(place, transactions, tx_product, tx_count, w_msg, mine):
    peers = 16
    slots = transactions.shape[0] // peers
    block = (4, mine, LANES)
    out = call(
        message_kernel,
        [(4, slots + PAD, LANES)] * 4 + [(4, slots, LANES)] * 4,
        (transactions, tx_product.reshape(-1, LANES), w_msg),
        smem=(place, tx_count),
    )

    def near(blocks):
        return [blocks[0]] + [swap(blocks[m], "hash", m, peers) for m in (1, 2, 3)]

    def rest(send, keep):
        parts = call(pair_kernel, [(mine, LANES)] * 4, (keep, swap(send, "tm", 1, 2)), smem=(place,))
        return [parts[0]] + [swap(parts[k], "hash", 4 * k, peers) for k in (1, 2, 3)]

    *first, ids = call(first_sum_kernel, [block, block, (8, LANES)], near(out[:4]), smem=(place,))
    second = call(second_sum_kernel, [block, block], (ids, *near(out[4:])), smem=(place,))
    return rest(*first) + rest(*second)


def gathered_plainly(transactions, tx_product, tx_count, w_msg, mine):
    peers, pair = lax.axis_size("hash"), lax.axis_size("tm")
    width = transactions.shape[1]
    slots = transactions.shape[0] // peers
    slot_index = lax.broadcasted_iota(jnp.int32, (peers, slots), 1)
    ids = jnp.where(slot_index < tx_count[:, None], tx_product.reshape(peers, slots), -1)
    outgoing = jax.nn.relu(jnp.dot(transactions, w_msg, precision=high))
    arrived = spread(outgoing.reshape(peers, slots, width)).reshape(-1, width)
    flat = spread(ids).reshape(-1)

    def part_sum(part):
        onehot = (flat[None, :] == (part * mine + lax.iota(jnp.int32, mine))[:, None]).astype(f32)
        return jnp.dot(onehot, arrived, precision=high)

    parts = lax.map(part_sum, jnp.arange(pair)).reshape(pair * mine, width)
    total = lax.psum_scatter(parts, "tm", scatter_dimension=0, tiled=True)
    return [total[:, :LANES], total[:, LANES:]]


def local(
    transactions,
    tx_product,
    tx_count,
    products,
    customers,
    send_rows,
    send_count,
    recv_customer,
    w_msg,
    w_prod_self,
    w_prod_agg,
    w_cust_self,
    w_cust_prod,
):
    peers, pair = lax.axis_size("hash"), lax.axis_size("tm")
    width = transactions.shape[1]
    mine = products.shape[0]
    send_slots = send_rows.shape[0] // peers
    place = jnp.stack([lax.axis_index("hash"), lax.axis_index("tm")]).astype(jnp.int32)

    if peers == 16 and pair == 2:
        parts = gathered_by_permutes(place, transactions, tx_product, tx_count, w_msg, mine)
    else:
        parts = gathered_plainly(transactions, tx_product, tx_count, w_msg, mine)

    product_self = jnp.dot(products, w_prod_self, precision=high)
    customer_self = jnp.dot(customers, w_cust_self, precision=high)
    send_index = lax.broadcasted_iota(jnp.int32, (peers, send_slots), 1)
    named = jnp.where(send_index < send_count[:, None], send_rows.reshape(peers, send_slots), -1).reshape(-1)
    picks = (named[:, None] == lax.iota(jnp.int32, mine)[None, :]).astype(bf16)
    incidence = (recv_customer[None, :] == lax.iota(jnp.int32, customers.shape[0])[:, None]).astype(bf16)

    new_products, listed = call(
        update_kernel,
        [products.shape, (peers, send_slots, width)],
        (*parts, product_self, products, *split_outside(w_prod_agg), picks),
    )
    incoming = spread(listed).reshape(-1, width)
    (new_customers,) = call(
        final_kernel,
        [customers.shape],
        (incoming, incidence, customer_self, customers, *split_outside(w_cust_prod)),
    )
    return new_products, new_customers


def solution(mesh):
    rows, flat = P(("hash", "tm"), None), P(("hash", "tm"))
    placed = (rows, flat, flat, rows, rows, flat, flat, flat, P(), P(), P(), P(), P())
    return jax.shard_map(local, mesh=mesh, in_specs=placed, out_specs=(rows, rows), check_vma=False)
```

```python
import jax
import jax.numpy as jnp
from jax import lax
from jax.experimental import pallas as pl
from jax.experimental.pallas import tpu as pltpu
from jax.sharding import PartitionSpec as P

high = lax.Precision.HIGH
f32, bf16 = jnp.float32, jnp.bfloat16
LANES = 128
PAD = 8


def split(x):
    top = x.astype(bf16)
    return top, (x - top.astype(f32)).astype(bf16)


def split_outside(x):
    top = lax.reduce_precision(x, 8, 7)
    return top.astype(bf16), (x - top).astype(bf16)


def mm(a, b):
    return jnp.dot(a, b, preferred_element_type=f32)


def dot3(x, w_top, w_low):
    top, low = split(x)
    return mm(top, w_top) + (mm(low, w_top) + mm(top, w_low))


def dot2(picks, x):
    top, low = split(x)
    return mm(picks, top) + mm(picks, low)


def call(kernel, out, ins, smem=(), space=pltpu.VMEM, scratch=()):
    vmem = pl.BlockSpec(memory_space=pltpu.VMEM)
    scalar = pl.BlockSpec(memory_space=pltpu.SMEM)
    return pl.pallas_call(
        kernel,
        out_shape=[jax.ShapeDtypeStruct(s, f32) for s in out],
        in_specs=[scalar] * len(smem) + [pl.BlockSpec(memory_space=space)] * len(ins),
        out_specs=[vmem] * len(out),
        scratch_shapes=list(scratch),
        compiler_params=pltpu.CompilerParams(vmem_limit_bytes=32 * 1024 * 1024),
    )(*smem, *ins)


def lanes():
    return lax.broadcasted_iota(jnp.int32, (1, LANES), 1)


def message_kernel(place, count, tx, ids, w, p0, p1, p2, p3, q0, q1, q2, q3, buf, w_buf, ids_buf, sem):
    near = place[0] & 3
    slots = q0.shape[1]
    copies = [pltpu.make_async_copy(w, w_buf, sem.at[4]), pltpu.make_async_copy(ids, ids_buf, sem.at[5])]
    order = (2, 3, 1, 0)
    copies += [pltpu.make_async_copy(tx.at[:, near ^ m], buf.at[m], sem.at[m]) for m in order]
    for copy in copies:
        copy.start()
    lane = lanes()
    copies[0].wait()
    copies[1].wait()
    w_top, w_low = split(w_buf[...])
    outs = ((p0, q0), (p1, q1), (p2, q2), (p3, q3))
    for m, copy in zip(order, copies[2:]):
        first, second = outs[m]
        c = near ^ m
        copy.wait()
        y = jnp.maximum(dot3(buf[m].reshape(4 * slots, 2 * LANES), w_top, w_low), 0.0)
        first[:, :slots, :] = y[:, :LANES].reshape(4, slots, LANES)
        second[...] = y[:, LANES:].reshape(4, slots, LANES)
        for z in range(4):
            row = ids_buf[pl.ds(2 * z + (c >> 1), 1), :]
            turned = pltpu.roll(row, slots, 1)
            twice = jnp.where((lane >= slots).astype(jnp.int32) == (c & 1), row, turned)
            twice = jnp.where((lane & (slots - 1)) < count[4 * z + c], twice, -1).astype(f32)
            first[z, slots:, :] = jnp.broadcast_to(twice, (PAD, LANES))


def sums(place, rows, blocks, send, keep):
    mine = send.shape[1]
    slots = LANES // 2
    own = place[1]
    row = lax.broadcasted_iota(jnp.int32, (2 * mine, LANES), 0)
    target = jnp.where(row < mine, row + (1 - own) * mine, row - mine + own * mine).astype(f32)
    for z in range(4):
        picks = jnp.concatenate([(r == target).astype(bf16) for r in rows[z]], 1)
        top, low = split(jnp.concatenate([block[z, :slots, :] for block in blocks], 0))
        total = mm(picks, jnp.concatenate([top, low], 1))
        total = total[:, :LANES] + total[:, LANES:]
        send[z] = total[:mine]
        keep[z] = total[mine:]


def first_sum_kernel(place, r0, r1, r2, r3, send, keep, ids):
    slots = r0.shape[1] - PAD
    lane = lanes()
    rows = []
    for z in range(4):
        one = [block[z, pl.ds(slots, 1), :] for block in (r0, r1, r2, r3)]
        rows.append([jnp.where(lane < slots, one[i], one[i + 1]) for i in (0, 2)])
        for i in range(2):
            ids[pl.ds(2 * z + i, 1), :] = rows[z][i]
    sums(place, rows, (r0, r1, r2, r3), send, keep)


def second_sum_kernel(place, ids, r0, r1, r2, r3, send, keep):
    rows = [[ids[pl.ds(2 * z + i, 1), :] for i in range(2)] for z in range(4)]
    sums(place, rows, (r0, r1, r2, r3), send, keep)


def pair_kernel(place, keep, got, b0, b1, b2, b3):
    far = place[0] >> 2
    for k, out in enumerate((b0, b1, b2, b3)):
        out[...] = keep[far ^ k] + got[far ^ k]


def update_kernel(*refs):
    parts, (own, table, w_top, w_low, picks, new, listed) = refs[:-7], refs[-7:]
    n = len(parts) // 2
    halves = [sum(part[...] for part in side) for side in (parts[:n], parts[n:])]
    gathered = jnp.concatenate(halves, 1)
    fresh = table[...] + jnp.maximum(own[...] + dot3(gathered, w_top[...], w_low[...]), 0.0)
    new[...] = fresh
    listed[...] = dot2(picks[...], fresh).reshape(listed.shape)


def final_kernel(incoming, incidence, own, table, w_top, w_low, new):
    bought = dot2(incidence[...], incoming[...])
    new[...] = table[...] + jnp.maximum(own[...] + dot3(bought, w_top[...], w_low[...]), 0.0)


def swap(x, axis, mask, size):
    return lax.ppermute(x, axis, [(i, i ^ mask) for i in range(size)])


def spread(x):
    return lax.all_to_all(x, "hash", split_axis=0, concat_axis=0, tiled=True)


def gathered_by_permutes(place, transactions, tx_product, tx_count, w_msg, mine):
    peers = 16
    slots = transactions.shape[0] // peers
    block = (4, mine, LANES)
    width = 2 * LANES
    out = call(
        message_kernel,
        [(4, slots + PAD, LANES)] * 4 + [(4, slots, LANES)] * 4,
        (transactions.reshape(4, 4, slots, width), tx_product.reshape(-1, LANES), w_msg),
        smem=(place, tx_count),
        space=pltpu.HBM,
        scratch=[
            pltpu.VMEM((4, 4, slots, width), f32),
            pltpu.VMEM((width, width), f32),
            pltpu.VMEM((peers * slots // LANES, LANES), jnp.int32),
            pltpu.SemaphoreType.DMA((6,)),
        ],
    )

    def near(blocks):
        return [blocks[0]] + [swap(blocks[m], "hash", m, peers) for m in (1, 2, 3)]

    def across(keep, got):
        parts = call(pair_kernel, [(mine, LANES)] * 4, (keep, got), smem=(place,))
        return [parts[0]] + [swap(parts[k], "hash", 4 * k, peers) for k in (1, 2, 3)]

    first, second = near(out[:4]), near(out[4:])
    send_p, keep_p, ids = call(first_sum_kernel, [block, block, (8, LANES)], first, smem=(place,))
    got_p = swap(send_p, "tm", 1, 2)
    got_p, *second = lax.optimization_barrier((got_p, *second))
    send_q, keep_q = call(second_sum_kernel, [block, block], (ids, *second), smem=(place,))
    got_p, send_q = lax.optimization_barrier((got_p, send_q))
    got_q = swap(send_q, "tm", 1, 2)
    return across(keep_p, got_p) + across(keep_q, got_q)


def gathered_plainly(transactions, tx_product, tx_count, w_msg, mine):
    peers, pair = lax.axis_size("hash"), lax.axis_size("tm")
    width = transactions.shape[1]
    slots = transactions.shape[0] // peers
    slot_index = lax.broadcasted_iota(jnp.int32, (peers, slots), 1)
    ids = jnp.where(slot_index < tx_count[:, None], tx_product.reshape(peers, slots), -1)
    outgoing = jax.nn.relu(jnp.dot(transactions, w_msg, precision=high))
    arrived = spread(outgoing.reshape(peers, slots, width)).reshape(-1, width)
    flat = spread(ids).reshape(-1)

    def part_sum(part):
        onehot = (flat[None, :] == (part * mine + lax.iota(jnp.int32, mine))[:, None]).astype(f32)
        return jnp.dot(onehot, arrived, precision=high)

    parts = lax.map(part_sum, jnp.arange(pair)).reshape(pair * mine, width)
    total = lax.psum_scatter(parts, "tm", scatter_dimension=0, tiled=True)
    return [total[:, :LANES], total[:, LANES:]]


def local(
    transactions,
    tx_product,
    tx_count,
    products,
    customers,
    send_rows,
    send_count,
    recv_customer,
    w_msg,
    w_prod_self,
    w_prod_agg,
    w_cust_self,
    w_cust_prod,
):
    peers, pair = lax.axis_size("hash"), lax.axis_size("tm")
    width = transactions.shape[1]
    mine = products.shape[0]
    send_slots = send_rows.shape[0] // peers
    place = jnp.stack([lax.axis_index("hash"), lax.axis_index("tm")]).astype(jnp.int32)

    if peers == 16 and pair == 2:
        parts = gathered_by_permutes(place, transactions, tx_product, tx_count, w_msg, mine)
    else:
        parts = gathered_plainly(transactions, tx_product, tx_count, w_msg, mine)

    product_self = jnp.dot(products, w_prod_self, precision=high)
    customer_self = jnp.dot(customers, w_cust_self, precision=high)
    send_index = lax.broadcasted_iota(jnp.int32, (peers, send_slots), 1)
    named = jnp.where(send_index < send_count[:, None], send_rows.reshape(peers, send_slots), -1).reshape(-1)
    picks = (named[:, None] == lax.iota(jnp.int32, mine)[None, :]).astype(bf16)
    incidence = (recv_customer[None, :] == lax.iota(jnp.int32, customers.shape[0])[:, None]).astype(bf16)

    new_products, listed = call(
        update_kernel,
        [products.shape, (peers, send_slots, width)],
        (*parts, product_self, products, *split_outside(w_prod_agg), picks),
    )
    incoming = spread(listed).reshape(-1, width)
    (new_customers,) = call(
        final_kernel,
        [customers.shape],
        (incoming, incidence, customer_self, customers, *split_outside(w_cust_prod)),
    )
    return new_products, new_customers


def solution(mesh):
    rows, flat = P(("hash", "tm"), None), P(("hash", "tm"))
    placed = (rows, flat, flat, rows, rows, flat, flat, flat, P(), P(), P(), P(), P())
    return jax.shard_map(local, mesh=mesh, in_specs=placed, out_specs=(rows, rows), check_vma=False)
```

```python
import jax
import jax.numpy as jnp
from jax import lax
from jax.experimental import pallas as pl
from jax.experimental.pallas import tpu as pltpu
from jax.sharding import PartitionSpec as P

high = lax.Precision.HIGH
f32, bf16 = jnp.float32, jnp.bfloat16
LANES = 128
PAD = 8


def split(x):
    top = x.astype(bf16)
    return top, (x - top.astype(f32)).astype(bf16)


def split_outside(x):
    top = lax.reduce_precision(x, 8, 7)
    return top.astype(bf16), (x - top).astype(bf16)


def mm(a, b):
    return jnp.dot(a, b, preferred_element_type=f32)


def dot3(x, w_top, w_low):
    top, low = split(x)
    return mm(top, w_top) + (mm(low, w_top) + mm(top, w_low))


def dot2(picks, x):
    top, low = split(x)
    return mm(picks, top) + mm(picks, low)


def call(kernel, out, ins, smem=()):
    vmem = pl.BlockSpec(memory_space=pltpu.VMEM)
    scalar = pl.BlockSpec(memory_space=pltpu.SMEM)
    return pl.pallas_call(
        kernel,
        out_shape=[jax.ShapeDtypeStruct(s, f32) for s in out],
        in_specs=[scalar] * len(smem) + [vmem] * len(ins),
        out_specs=[vmem] * len(out),
        compiler_params=pltpu.CompilerParams(vmem_limit_bytes=32 * 1024 * 1024),
    )(*smem, *ins)


def lanes():
    return lax.broadcasted_iota(jnp.int32, (1, LANES), 1)


def message_kernel(place, count, tx, ids, w_top, w_low, own, core, l2, l3, r2, r3, b2, b3):
    near, far = place[0] & 3, place[0] >> 2
    slots = tx.shape[0] // 16
    lane = lanes()
    top, low = w_top[...], w_low[...]
    for m in (2, 3, 1, 0):
        c = near ^ m
        buckets = [4 * (far ^ k) + c for k in (2, 3, 1, 0)]
        x = jnp.concatenate([tx[pl.ds(pl.multiple_of(b * slots, slots), slots), :] for b in buckets], 0)
        y = jnp.maximum(dot3(x, top, low), 0.0).reshape(4, slots, 2 * LANES)
        if m < 2:
            outs = ((own, core)[m], 0, 0), ((own, core)[m], 0, slots), ((own, core)[m], 2, 0)
        else:
            outs = ((l2, l3)[m - 2], 0, 0), ((r2, r3)[m - 2], 0, 0), ((b2, b3)[m - 2], 0, 0)
        (left, _, _), (right, _, at), (both, first, _) = outs
        left[:2, :slots, :] = y[:2, :, :LANES]
        right[:2, at : at + slots, :] = y[:2, :, LANES:]
        both[first : first + 2, :slots, :] = y[2:, :, :LANES]
        both[first : first + 2, slots : 2 * slots, :] = y[2:, :, LANES:]
        for i, b in enumerate(buckets):
            row = ids[pl.ds(b >> 1, 1), :]
            turned = pltpu.roll(row, slots, 1)
            twice = jnp.where((lane >= slots).astype(jnp.int32) == (c & 1), row, turned)
            twice = jnp.where((lane & (slots - 1)) < count[b], twice, -1).astype(f32)
            target, z = (left, i) if i < 2 else (both, first + i - 2)
            target[z, target.shape[1] - PAD :, :] = jnp.broadcast_to(twice, (PAD, LANES))


def id_rows(blocks, starts):
    lane = lanes()
    rows = []
    for z in range(2):
        one = [block[start + z, pl.ds(block.shape[1] - PAD, 1), :] for block, start in zip(blocks, starts)]
        rows.append([jnp.where(lane < LANES // 2, one[i], one[i + 1]) for i in (0, 2)])
    return rows


def sums(place, rows, sides, send, keep):
    mine = send.shape[1]
    slots = LANES // 2
    own = place[1]
    row = lax.broadcasted_iota(jnp.int32, (2 * mine, LANES), 0)
    target = jnp.where(row < mine, row + (1 - own) * mine, row - mine + own * mine).astype(f32)
    for z in range(2):
        picks = jnp.concatenate([(r == target).astype(bf16) for r in rows[z]], 1)
        for side, blocks in enumerate(sides):
            x = jnp.concatenate([block[first + z, at : at + slots, :] for block, first, at in blocks], 0)
            total = mm(picks, jnp.concatenate(split(x), 1))
            total = total[:, :LANES] + total[:, LANES:]
            send[z, :, side * LANES : (side + 1) * LANES] = total[:mine]
            keep[z, :, side * LANES : (side + 1) * LANES] = total[mine:]


def left_kernel(place, own, core, l2, l3, send, keep, ids):
    blocks = (own, core, l2, l3)
    rows = id_rows(blocks, (0, 0, 0, 0))
    for z in range(2):
        for i in range(2):
            ids[pl.ds(2 * z + i, 1), :] = rows[z][i]
    sums(place, rows, [[(block, 0, 0) for block in blocks]], send, keep)


def right_kernel(place, ids, own, core, r2, r3, send, keep):
    rows = [[ids[pl.ds(2 * z + i, 1), :] for i in range(2)] for z in range(2)]
    slots = r2.shape[1]
    sums(place, rows, [[(own, 0, slots), (core, 0, slots), (r2, 0, 0), (r3, 0, 0)]], send, keep)


def both_kernel(place, own, core, b2, b3, send, keep):
    blocks, starts = (own, core, b2, b3), (2, 2, 0, 0)
    slots = LANES // 2
    sides = [[(block, first, at) for block, first in zip(blocks, starts)] for at in (0, slots)]
    sums(place, id_rows(blocks, starts), sides, send, keep)


def pair_kernel(keep, got, first, second):
    first[...] = keep[0] + got[0]
    second[...] = keep[1] + got[1]


def update_kernel(*refs):
    parts, (own, table, w_top, w_low, picks, new, listed) = refs[:-7], refs[-7:]
    wide = [part[...] for part in parts if part.shape[1] != LANES]
    left, right = (sum(part[...] for part in side) for side in (parts[:2], parts[2:4]))
    gathered = jnp.concatenate([left, right], 1) + sum(wide)
    fresh = table[...] + jnp.maximum(own[...] + dot3(gathered, w_top[...], w_low[...]), 0.0)
    new[...] = fresh
    listed[...] = dot2(picks[...], fresh).reshape(listed.shape)


def final_kernel(incoming, incidence, own, table, w_top, w_low, new):
    bought = dot2(incidence[...], incoming[...])
    new[...] = table[...] + jnp.maximum(own[...] + dot3(bought, w_top[...], w_low[...]), 0.0)


def swap(x, axis, mask, size):
    return lax.ppermute(x, axis, [(i, i ^ mask) for i in range(size)])


def spread(x):
    return lax.all_to_all(x, "hash", split_axis=0, concat_axis=0, tiled=True)


def gathered_by_permutes(place, transactions, tx_product, tx_count, w_msg, mine):
    peers = 16
    slots = transactions.shape[0] // peers
    own, core, *out = call(
        message_kernel,
        [(4, 2 * slots + PAD, LANES)] * 2
        + [(2, slots + PAD, LANES)] * 2
        + [(2, slots, LANES)] * 2
        + [(2, 2 * slots + PAD, LANES)] * 2,
        (transactions, tx_product.reshape(-1, LANES), *split_outside(w_msg)),
        smem=(place, tx_count),
    )
    half, whole = (2, mine, LANES), (2, mine, 2 * LANES)

    def near(blocks):
        return [swap(block, "hash", mask, peers) for block, mask in zip(blocks, (2, 3))]

    def pair(keep, got):
        return call(pair_kernel, [keep.shape[1:]] * 2, (keep, got))

    def after(value, ready):
        return lax.optimization_barrier((*value, *ready))[: len(value)]

    def across(parts):
        return [swap(part, "hash", mask, peers) for part, mask in zip(parts, (8, 12))]

    left, right = near(out[:2]), near(out[2:4])
    core = swap(core, "hash", 1, peers)
    both = near(after(out[4:], left))
    send_l, keep_l, ids = call(left_kernel, [half, half, (8, LANES)], (own, core, *left), smem=(place,))
    got_l = swap(send_l, "tm", 1, 2)
    send_r, keep_r = call(right_kernel, [half, half], (ids, own, core, *after(right, [got_l])), smem=(place,))
    got_r = swap(send_r, "tm", 1, 2)
    parts_l = pair(keep_l, *after([got_l], [send_r]))
    far_l = across(parts_l)
    send_b, keep_b = call(both_kernel, [whole, whole], (own, core, *after(both, [got_r, *parts_l])), smem=(place,))
    got_b = swap(send_b, "tm", 1, 2)
    far_r = across(pair(keep_r, *after([got_r], [send_b])))
    next_to, mine_b = pair(keep_b, *after([got_b], far_l))
    return [*far_l, *far_r, swap(next_to, "hash", 4, peers), mine_b]


def gathered_plainly(transactions, tx_product, tx_count, w_msg, mine):
    peers, pair = lax.axis_size("hash"), lax.axis_size("tm")
    width = transactions.shape[1]
    slots = transactions.shape[0] // peers
    slot_index = lax.broadcasted_iota(jnp.int32, (peers, slots), 1)
    ids = jnp.where(slot_index < tx_count[:, None], tx_product.reshape(peers, slots), -1)
    outgoing = jax.nn.relu(jnp.dot(transactions, w_msg, precision=high))
    arrived = spread(outgoing.reshape(peers, slots, width)).reshape(-1, width)
    flat = spread(ids).reshape(-1)

    def part_sum(part):
        onehot = (flat[None, :] == (part * mine + lax.iota(jnp.int32, mine))[:, None]).astype(f32)
        return jnp.dot(onehot, arrived, precision=high)

    parts = lax.map(part_sum, jnp.arange(pair)).reshape(pair * mine, width)
    total = lax.psum_scatter(parts, "tm", scatter_dimension=0, tiled=True)
    zero = jnp.zeros((mine, LANES), f32)
    return [zero, zero, zero, zero, total]


def local(
    transactions,
    tx_product,
    tx_count,
    products,
    customers,
    send_rows,
    send_count,
    recv_customer,
    w_msg,
    w_prod_self,
    w_prod_agg,
    w_cust_self,
    w_cust_prod,
):
    peers, pair = lax.axis_size("hash"), lax.axis_size("tm")
    width = transactions.shape[1]
    mine = products.shape[0]
    send_slots = send_rows.shape[0] // peers
    place = jnp.stack([lax.axis_index("hash"), lax.axis_index("tm")]).astype(jnp.int32)

    if peers == 16 and pair == 2:
        parts = gathered_by_permutes(place, transactions, tx_product, tx_count, w_msg, mine)
    else:
        parts = gathered_plainly(transactions, tx_product, tx_count, w_msg, mine)

    product_self = jnp.dot(products, w_prod_self, precision=high)
    customer_self = jnp.dot(customers, w_cust_self, precision=high)
    send_index = lax.broadcasted_iota(jnp.int32, (peers, send_slots), 1)
    named = jnp.where(send_index < send_count[:, None], send_rows.reshape(peers, send_slots), -1).reshape(-1)
    picks = (named[:, None] == lax.iota(jnp.int32, mine)[None, :]).astype(bf16)
    incidence = (recv_customer[None, :] == lax.iota(jnp.int32, customers.shape[0])[:, None]).astype(bf16)

    new_products, listed = call(
        update_kernel,
        [products.shape, (peers, send_slots, width)],
        (*parts, product_self, products, *split_outside(w_prod_agg), picks),
    )
    incoming = spread(listed).reshape(-1, width)
    (new_customers,) = call(
        final_kernel,
        [customers.shape],
        (incoming, incidence, customer_self, customers, *split_outside(w_cust_prod)),
    )
    return new_products, new_customers


def solution(mesh):
    rows, flat = P(("hash", "tm"), None), P(("hash", "tm"))
    placed = (rows, flat, flat, rows, rows, flat, flat, flat, P(), P(), P(), P(), P())
    return jax.shard_map(local, mesh=mesh, in_specs=placed, out_specs=(rows, rows), check_vma=False)
```

```python
import functools

import jax
import jax.numpy as jnp
from jax import lax
from jax.experimental import pallas as pl
from jax.experimental.pallas import tpu as pltpu
from jax.sharding import PartitionSpec as P

high = lax.Precision.HIGH
f32, bf16 = jnp.float32, jnp.bfloat16
LANES = 128
PAD = 8


def split(x):
    top = x.astype(bf16)
    return top, (x - top.astype(f32)).astype(bf16)


def split_outside(x):
    top = lax.reduce_precision(x, 8, 7)
    return top.astype(bf16), (x - top).astype(bf16)


def mm(a, b):
    return jnp.dot(a, b, preferred_element_type=f32)


def dot3(x, w_top, w_low):
    top, low = split(x)
    return mm(top, w_top) + (mm(low, w_top) + mm(top, w_low))


def dot2(picks, x):
    top, low = split(x)
    return mm(picks, top) + mm(picks, low)


def call(kernel, out, ins, smem=()):
    vmem = pl.BlockSpec(memory_space=pltpu.VMEM)
    scalar = pl.BlockSpec(memory_space=pltpu.SMEM)
    return pl.pallas_call(
        kernel,
        out_shape=[jax.ShapeDtypeStruct(s, f32) for s in out],
        in_specs=[scalar] * len(smem) + [vmem] * len(ins),
        out_specs=[vmem] * len(out),
        compiler_params=pltpu.CompilerParams(vmem_limit_bytes=32 * 1024 * 1024),
    )(*smem, *ins)


def lanes():
    return lax.broadcasted_iota(jnp.int32, (1, LANES), 1)


def message_kernel(place, count, tx, ids, w_top, w_low, own, core, l2, l3, r2, r3, b2, b3):
    near, far = place[0] & 3, place[0] >> 2
    slots = tx.shape[0] // 16
    lane = lanes()
    top, low = w_top[...], w_low[...]
    for m in (2, 3, 1, 0):
        c = near ^ m
        buckets = [4 * (far ^ k) + c for k in (2, 3, 1, 0)]
        x = jnp.concatenate([tx[pl.ds(pl.multiple_of(b * slots, slots), slots), :] for b in buckets], 0)
        y = jnp.maximum(dot3(x, top, low), 0.0).reshape(4, slots, 2 * LANES)
        if m < 2:
            outs = ((own, core)[m], 0, 0), ((own, core)[m], 0, slots), ((own, core)[m], 2, 0)
        else:
            outs = ((l2, l3)[m - 2], 0, 0), ((r2, r3)[m - 2], 0, 0), ((b2, b3)[m - 2], 0, 0)
        (left, _, _), (right, _, at), (both, first, _) = outs
        left[:2, :slots, :] = y[:2, :, :LANES]
        right[:2, at : at + slots, :] = y[:2, :, LANES:]
        both[first : first + 2, :slots, :] = y[2:, :, :LANES]
        both[first : first + 2, slots : 2 * slots, :] = y[2:, :, LANES:]
        for i, b in enumerate(buckets):
            row = ids[pl.ds(b >> 1, 1), :]
            turned = pltpu.roll(row, slots, 1)
            twice = jnp.where((lane >= slots).astype(jnp.int32) == (c & 1), row, turned)
            twice = jnp.where((lane & (slots - 1)) < count[b], twice, -1).astype(f32)
            target, z = (left, i) if i < 2 else (both, first + i - 2)
            target[z, target.shape[1] - PAD :, :] = jnp.broadcast_to(twice, (PAD, LANES))


def id_rows(blocks, starts):
    lane = lanes()
    rows = []
    for z in range(2):
        one = [block[start + z, pl.ds(block.shape[1] - PAD, 1), :] for block, start in zip(blocks, starts)]
        rows.append([jnp.where(lane < LANES // 2, one[i], one[i + 1]) for i in (0, 2)])
    return rows


def sums(place, rows, sides, send, keep):
    mine = send.shape[1]
    slots = LANES // 2
    own = place[1]
    row = lax.broadcasted_iota(jnp.int32, (2 * mine, LANES), 0)
    target = jnp.where(row < mine, row + (1 - own) * mine, row - mine + own * mine).astype(f32)
    for z in range(2):
        picks = jnp.concatenate([(r == target).astype(bf16) for r in rows[z]], 1)
        for side, blocks in enumerate(sides):
            x = jnp.concatenate([block[first + z, at : at + slots, :] for block, first, at in blocks], 0)
            total = mm(picks, jnp.concatenate(split(x), 1))
            total = total[:, :LANES] + total[:, LANES:]
            send[z, :, side * LANES : (side + 1) * LANES] = total[:mine]
            keep[z, :, side * LANES : (side + 1) * LANES] = total[mine:]


def left_kernel(place, own, core, l2, l3, send, keep, ids):
    blocks = (own, core, l2, l3)
    rows = id_rows(blocks, (0, 0, 0, 0))
    for z in range(2):
        for i in range(2):
            ids[pl.ds(2 * z + i, 1), :] = rows[z][i]
    sums(place, rows, [[(block, 0, 0) for block in blocks]], send, keep)


def right_kernel(place, ids, own, core, r2, r3, send, keep):
    rows = [[ids[pl.ds(2 * z + i, 1), :] for i in range(2)] for z in range(2)]
    slots = r2.shape[1]
    sums(place, rows, [[(own, 0, slots), (core, 0, slots), (r2, 0, 0), (r3, 0, 0)]], send, keep)


def both_kernel(place, own, core, b2, b3, send, keep):
    blocks, starts = (own, core, b2, b3), (2, 2, 0, 0)
    slots = LANES // 2
    sides = [[(block, first, at) for block, first in zip(blocks, starts)] for at in (0, slots)]
    sums(place, id_rows(blocks, starts), sides, send, keep)


def pair_kernel(keep, got, first, second):
    first[...] = keep[0] + got[0]
    second[...] = keep[1] + got[1]


def update_kernel(n, *refs):
    parts, (own, table, w_top, w_low, picks), (new, *outs) = refs[:n], refs[n : n + 5], refs[n + 5 :]
    wide = [part[...] for part in parts if part.shape[1] != LANES]
    left, right = (sum(part[...] for part in side) for side in (parts[:2], parts[2:4]))
    gathered = jnp.concatenate([left, right], 1) + sum(wide)
    fresh = table[...] + jnp.maximum(own[...] + dot3(gathered, w_top[...], w_low[...]), 0.0)
    new[...] = fresh
    listed = dot2(picks[...], fresh)
    at = 0
    for out in outs:
        rows = out.shape[0] * out.shape[1]
        out[...] = listed[at : at + rows].reshape(out.shape)
        at += rows


def turn_kernel(start, own, core, third, fourth, first, second):
    for i, out in enumerate((first, second)):
        for m, (block, at) in enumerate(((own, start), (core, start), (third, 0), (fourth, 0))):
            out[m] = block[at + i]


def final_kernel(incidence, own, table, w_top, w_low, *refs):
    incoming, new = refs[:-1], refs[-1]
    width = table.shape[1]
    rows = jnp.concatenate([block[...].reshape(-1, width) for block in incoming], 0)
    bought = dot2(incidence[...], rows)
    new[...] = table[...] + jnp.maximum(own[...] + dot3(bought, w_top[...], w_low[...]), 0.0)


def swap(x, axis, mask, size):
    return lax.ppermute(x, axis, [(i, i ^ mask) for i in range(size)])


def spread(x):
    return lax.all_to_all(x, "hash", split_axis=0, concat_axis=0, tiled=True)


def gathered_by_permutes(place, transactions, tx_product, tx_count, w_msg, mine):
    peers = 16
    slots = transactions.shape[0] // peers
    own, core, *out = call(
        message_kernel,
        [(4, 2 * slots + PAD, LANES)] * 2
        + [(2, slots + PAD, LANES)] * 2
        + [(2, slots, LANES)] * 2
        + [(2, 2 * slots + PAD, LANES)] * 2,
        (transactions, tx_product.reshape(-1, LANES), *split_outside(w_msg)),
        smem=(place, tx_count),
    )
    half, whole = (2, mine, LANES), (2, mine, 2 * LANES)

    def near(blocks):
        return [swap(block, "hash", mask, peers) for block, mask in zip(blocks, (2, 3))]

    def pair(keep, got):
        return call(pair_kernel, [keep.shape[1:]] * 2, (keep, got))

    def after(value, ready):
        return lax.optimization_barrier((*value, *ready))[: len(value)]

    def across(parts):
        return [swap(part, "hash", mask, peers) for part, mask in zip(parts, (8, 12))]

    left, right = near(out[:2]), near(out[2:4])
    core = swap(core, "hash", 1, peers)
    both = near(after(out[4:], left))
    send_l, keep_l, ids = call(left_kernel, [half, half, (8, LANES)], (own, core, *left), smem=(place,))
    got_l = swap(send_l, "tm", 1, 2)
    send_r, keep_r = call(right_kernel, [half, half], (ids, own, core, *after(right, [got_l])), smem=(place,))
    got_r = swap(send_r, "tm", 1, 2)
    parts_l = pair(keep_l, *after([got_l], [send_r]))
    far_l = across(parts_l)
    send_b, keep_b = call(both_kernel, [whole, whole], (own, core, *after(both, [got_r, *parts_l])), smem=(place,))
    got_b = swap(send_b, "tm", 1, 2)
    parts_r = pair(keep_r, *after([got_r], [send_b]))
    next_to, mine_b = pair(keep_b, *after([got_b], [*far_l, *parts_r]))
    return [*far_l, *across(parts_r), swap(next_to, "hash", 4, peers), mine_b]


def pick(x, i, axis):
    return lax.dynamic_index_in_dim(x, i, axis, keepdims=True)


def by_distance(x, place, zs):
    x = x.reshape(4, 4, -1)
    x = jnp.concatenate([pick(x, (place[0] >> 2) ^ k, 0) for k in zs], 0)
    return jnp.concatenate([pick(x, (place[0] & 3) ^ m, 1) for m in range(4)], 1)


def deliver(own, core, a2, a3, b2, b3):
    peers = 16
    turned = [(4, *own.shape[1:])] * 2
    a2, a3 = swap(a2, "hash", 2, peers), swap(a3, "hash", 3, peers)
    core = swap(core, "hash", 1, peers)
    b2, b3 = swap(b2, "hash", 2, peers), swap(b3, "hash", 3, peers)
    two, three = call(functools.partial(turn_kernel, 0), turned, (own, core, a2, a3))
    two, three = swap(two, "hash", 8, peers), swap(three, "hash", 12, peers)
    one, here = call(functools.partial(turn_kernel, 2), turned, (own, core, b2, b3))
    return [two, three, swap(one, "hash", 4, peers), here]


def gathered_plainly(transactions, tx_product, tx_count, w_msg, mine):
    peers, pair = lax.axis_size("hash"), lax.axis_size("tm")
    width = transactions.shape[1]
    slots = transactions.shape[0] // peers
    slot_index = lax.broadcasted_iota(jnp.int32, (peers, slots), 1)
    ids = jnp.where(slot_index < tx_count[:, None], tx_product.reshape(peers, slots), -1)
    outgoing = jax.nn.relu(jnp.dot(transactions, w_msg, precision=high))
    arrived = spread(outgoing.reshape(peers, slots, width)).reshape(-1, width)
    flat = spread(ids).reshape(-1)

    def part_sum(part):
        onehot = (flat[None, :] == (part * mine + lax.iota(jnp.int32, mine))[:, None]).astype(f32)
        return jnp.dot(onehot, arrived, precision=high)

    parts = lax.map(part_sum, jnp.arange(pair)).reshape(pair * mine, width)
    total = lax.psum_scatter(parts, "tm", scatter_dimension=0, tiled=True)
    zero = jnp.zeros((mine, LANES), f32)
    return [zero, zero, zero, zero, total]


def local(
    transactions,
    tx_product,
    tx_count,
    products,
    customers,
    send_rows,
    send_count,
    recv_customer,
    w_msg,
    w_prod_self,
    w_prod_agg,
    w_cust_self,
    w_cust_prod,
):
    peers, pair = lax.axis_size("hash"), lax.axis_size("tm")
    width = transactions.shape[1]
    mine = products.shape[0]
    send_slots = send_rows.shape[0] // peers
    place = jnp.stack([lax.axis_index("hash"), lax.axis_index("tm")]).astype(jnp.int32)

    if peers == 16 and pair == 2:
        parts = gathered_by_permutes(place, transactions, tx_product, tx_count, w_msg, mine)
    else:
        parts = gathered_plainly(transactions, tx_product, tx_count, w_msg, mine)

    product_self = jnp.dot(products, w_prod_self, precision=high)
    customer_self = jnp.dot(customers, w_cust_self, precision=high)
    send_index = lax.broadcasted_iota(jnp.int32, (peers, send_slots), 1)
    named = jnp.where(send_index < send_count[:, None], send_rows.reshape(peers, send_slots), -1)
    receivers = recv_customer.reshape(peers, send_slots)
    near = peers == 16 and pair == 2
    if near:
        order = (2, 3, 1, 0)
        named = by_distance(named, place, order).transpose(1, 0, 2)
        receivers = by_distance(receivers, place, order)
    picks = (named.reshape(-1)[:, None] == lax.iota(jnp.int32, mine)[None, :]).astype(bf16)
    incidence = (receivers.reshape(-1)[None, :] == lax.iota(jnp.int32, customers.shape[0])[:, None]).astype(bf16)

    counts = (4, 4, 2, 2, 2, 2) if near else (peers,)
    new_products, *listed = call(
        functools.partial(update_kernel, len(parts)),
        [products.shape] + [(n, send_slots, width) for n in counts],
        (*parts, product_self, products, *split_outside(w_prod_agg), picks),
    )
    if near:
        own, core, a2, b2, a3, b3 = listed
        incoming = deliver(own, core, a2, a3, b2, b3)
    else:
        incoming = [spread(listed[0])]
    (new_customers,) = call(
        final_kernel,
        [customers.shape],
        (incidence, customer_self, customers, *split_outside(w_cust_prod), *incoming),
    )
    return new_products, new_customers


def solution(mesh):
    rows, flat = P(("hash", "tm"), None), P(("hash", "tm"))
    placed = (rows, flat, flat, rows, rows, flat, flat, flat, P(), P(), P(), P(), P())
    return jax.shard_map(local, mesh=mesh, in_specs=placed, out_specs=(rows, rows), check_vma=False)
```

```python
import functools

import jax
import jax.numpy as jnp
from jax import lax
from jax.experimental import pallas as pl
from jax.experimental.pallas import tpu as pltpu
from jax.sharding import PartitionSpec as P

high = lax.Precision.HIGH
f32, bf16 = jnp.float32, jnp.bfloat16
LANES = 128
PAD = 8


def split(x):
    top = x.astype(bf16)
    return top, (x - top.astype(f32)).astype(bf16)


def split_outside(x):
    top = lax.reduce_precision(x, 8, 7)
    return top.astype(bf16), (x - top).astype(bf16)


def mm(a, b):
    return jnp.dot(a, b, preferred_element_type=f32)


def dot3(x, w_top, w_low):
    top, low = split(x)
    return mm(top, w_top) + (mm(low, w_top) + mm(top, w_low))


def dot2(picks, x):
    top, low = split(x)
    return mm(picks, top) + mm(picks, low)


def call(kernel, out, ins, smem=()):
    vmem = pl.BlockSpec(memory_space=pltpu.VMEM)
    scalar = pl.BlockSpec(memory_space=pltpu.SMEM)
    return pl.pallas_call(
        kernel,
        out_shape=[jax.ShapeDtypeStruct(s, f32) for s in out],
        in_specs=[scalar] * len(smem) + [vmem] * len(ins),
        out_specs=[vmem] * len(out),
        compiler_params=pltpu.CompilerParams(vmem_limit_bytes=32 * 1024 * 1024),
    )(*smem, *ins)


def lanes():
    return lax.broadcasted_iota(jnp.int32, (1, LANES), 1)


def message_kernel(place, count, tx, ids, w_top, w_low, own, core, l2, l3, r2, r3):
    near, far = place[0] & 3, place[0] >> 2
    slots = tx.shape[0] // 16
    lane = lanes()
    top, low = w_top[...], w_low[...]
    for m in (2, 3, 1, 0):
        c = near ^ m
        buckets = [4 * (far ^ k) + c for k in (2, 3, 1, 0)]
        x = jnp.concatenate([tx[pl.ds(pl.multiple_of(b * slots, slots), slots), :] for b in buckets], 0)
        y = jnp.maximum(dot3(x, top, low), 0.0)
        for i, b in enumerate(buckets):
            row = ids[pl.ds(b >> 1, 1), :]
            turned = pltpu.roll(row, slots, 1)
            twice = jnp.where((lane >= slots).astype(jnp.int32) == (c & 1), row, turned)
            twice = jnp.where((lane & (slots - 1)) < count[b], twice, -1).astype(f32)
            twice = jnp.broadcast_to(twice, (PAD, LANES))
            left, right = y[i * slots : (i + 1) * slots, :LANES], y[i * slots : (i + 1) * slots, LANES:]
            if m < 2:
                out = (own, core)[m]
                out[i, :slots, :] = left
                out[i, slots : 2 * slots, :] = right
                out[i, 2 * slots :, :] = twice
            elif i < 3:
                first, second = (l2, l3)[m - 2], (r2, r3)[m - 2]
                first[i, :slots, :] = left
                first[i, slots:, :] = twice
                second[i * slots : (i + 1) * slots, :] = right
            else:
                out = (r2, r3)[m - 2]
                out[3 * slots : 4 * slots, :] = left
                out[4 * slots : 5 * slots, :] = right
                out[5 * slots :, :] = twice


def targets(place, mine):
    row = lax.broadcasted_iota(jnp.int32, (2 * mine, LANES), 0)
    own = place[1]
    return jnp.where(row < mine, row + (1 - own) * mine, row - mine + own * mine).astype(f32)


def joined(one):
    lane = lanes()
    return [jnp.where(lane < LANES // 2, one[i], one[i + 1]) for i in (0, 2)]


def bucket_sum(rows, target, blocks, send, keep, at):
    mine = send.shape[1]
    picks = jnp.concatenate([(r == target).astype(bf16) for r in rows], 1)
    total = mm(picks, jnp.concatenate(split(jnp.concatenate(blocks, 0)), 1))
    total = total[:, :LANES] + total[:, LANES:]
    send[at] = total[:mine]
    keep[at] = total[mine:]


def left_kernel(place, own, core, l2, l3, send, keep, ids):
    target = targets(place, send.shape[1])
    senders = (own, core, l2, l3)
    slots = LANES // 2
    for z in range(3):
        rows = joined([block[z, pl.ds(block.shape[1] - PAD, 1), :] for block in senders])
        for i in range(2):
            ids[pl.ds(2 * z + i, 1), :] = rows[i]
        bucket_sum(rows, target, [block[z, :slots, :] for block in senders], send, keep, z)


def rest_kernel(place, ids, own, core, r2, r3, send, keep):
    target = targets(place, send.shape[1])
    slots = LANES // 2
    for z in range(3):
        rows = [ids[pl.ds(2 * z + i, 1), :] for i in range(2)]
        blocks = [block[z, slots : 2 * slots, :] for block in (own, core)]
        blocks += [block[z * slots : (z + 1) * slots, :] for block in (r2, r3)]
        bucket_sum(rows, target, blocks, send, keep, z)
    one = [block[3, pl.ds(2 * slots, 1), :] for block in (own, core)]
    rows = joined(one + [block[pl.ds(5 * slots, 1), :] for block in (r2, r3)])
    for side in range(2):
        blocks = [block[3, side * slots : (side + 1) * slots, :] for block in (own, core)]
        blocks += [block[(3 + side) * slots : (4 + side) * slots, :] for block in (r2, r3)]
        bucket_sum(rows, target, blocks, send, keep, 3 + side)


def pair_kernel(keep, got, *outs):
    for i in range(3):
        outs[i][...] = keep[i] + got[i]
    for own in outs[3:]:
        own[:, :LANES] = keep[3] + got[3]
        own[:, LANES:] = keep[4] + got[4]


def update_kernel(n, *refs):
    parts, (own, table, w_top, w_low, picks), (new, *outs) = refs[:n], refs[n : n + 5], refs[n + 5 :]
    wide = [part[...] for part in parts if part.shape[1] != LANES]
    left, right = (sum(part[...] for part in side) for side in (parts[:3], parts[3:6]))
    gathered = jnp.concatenate([left, right], 1) + sum(wide)
    fresh = table[...] + jnp.maximum(own[...] + dot3(gathered, w_top[...], w_low[...]), 0.0)
    new[...] = fresh
    listed = dot2(picks[...], fresh)
    at = 0
    for out in outs:
        rows = out.shape[0] * out.shape[1]
        out[...] = listed[at : at + rows].reshape(out.shape)
        at += rows


def turn_kernel(start, own, core, third, fourth, first, second):
    for i, out in enumerate((first, second)):
        for m, (block, at) in enumerate(((own, start), (core, start), (third, 0), (fourth, 0))):
            out[m] = block[at + i]


def final_kernel(incidence, own, table, w_top, w_low, *refs):
    incoming, new = refs[:-1], refs[-1]
    width = table.shape[1]
    rows = jnp.concatenate([block[...].reshape(-1, width) for block in incoming], 0)
    bought = dot2(incidence[...], rows)
    new[...] = table[...] + jnp.maximum(own[...] + dot3(bought, w_top[...], w_low[...]), 0.0)


def swap(x, axis, mask, size):
    return lax.ppermute(x, axis, [(i, i ^ mask) for i in range(size)])


def spread(x):
    return lax.all_to_all(x, "hash", split_axis=0, concat_axis=0, tiled=True)


def gathered_by_permutes(place, transactions, tx_product, tx_count, w_msg, mine):
    peers = 16
    slots = transactions.shape[0] // peers
    own, core, l2, l3, r2, r3 = call(
        message_kernel,
        [(4, 2 * slots + PAD, LANES)] * 2 + [(3, slots + PAD, LANES)] * 2 + [(5 * slots + PAD, LANES)] * 2,
        (transactions, tx_product.reshape(-1, LANES), *split_outside(w_msg)),
        smem=(place, tx_count),
    )
    left, rest, part = (3, mine, LANES), (5, mine, LANES), (mine, LANES)

    def near(blocks):
        return [swap(block, "hash", mask, peers) for block, mask in zip(blocks, (2, 3))]

    def across(parts):
        return [swap(part, "hash", mask, peers) for part, mask in zip(parts, (8, 12, 4))]

    def after(value, ready):
        return lax.optimization_barrier((*value, *ready))[: len(value)]

    first = near((l2, l3))
    core = swap(core, "hash", 1, peers)
    second = near(after((r2, r3), first))
    send_l, keep_l, ids = call(left_kernel, [left, left, (8, LANES)], (own, core, *first), smem=(place,))
    got_l = swap(send_l, "tm", 1, 2)
    send_r, keep_r = call(rest_kernel, [rest, rest], (ids, own, core, *after(second, [got_l])), smem=(place,))
    got_r = swap(send_r, "tm", 1, 2)
    far_l = across(call(pair_kernel, [part] * 3, (keep_l, *after([got_l], [send_r]))))
    *parts_r, whole = call(pair_kernel, [part] * 3 + [(mine, 2 * LANES)], (keep_r, *after([got_r], far_l)))
    return [*far_l, *across(parts_r), whole]


def pick(x, i, axis):
    return lax.dynamic_index_in_dim(x, i, axis, keepdims=True)


def by_distance(x, place, zs):
    x = x.reshape(4, 4, -1)
    x = jnp.concatenate([pick(x, (place[0] >> 2) ^ k, 0) for k in zs], 0)
    return jnp.concatenate([pick(x, (place[0] & 3) ^ m, 1) for m in range(4)], 1)


def deliver(own, core, a2, a3, b2, b3):
    peers = 16
    turned = [(4, *own.shape[1:])] * 2
    a2, a3 = swap(a2, "hash", 2, peers), swap(a3, "hash", 3, peers)
    core = swap(core, "hash", 1, peers)
    b2, b3 = swap(b2, "hash", 2, peers), swap(b3, "hash", 3, peers)
    two, three = call(functools.partial(turn_kernel, 0), turned, (own, core, a2, a3))
    two, three = swap(two, "hash", 8, peers), swap(three, "hash", 12, peers)
    one, here = call(functools.partial(turn_kernel, 2), turned, (own, core, b2, b3))
    return [two, three, swap(one, "hash", 4, peers), here]


def gathered_plainly(transactions, tx_product, tx_count, w_msg, mine):
    peers, pair = lax.axis_size("hash"), lax.axis_size("tm")
    width = transactions.shape[1]
    slots = transactions.shape[0] // peers
    slot_index = lax.broadcasted_iota(jnp.int32, (peers, slots), 1)
    ids = jnp.where(slot_index < tx_count[:, None], tx_product.reshape(peers, slots), -1)
    outgoing = jax.nn.relu(jnp.dot(transactions, w_msg, precision=high))
    arrived = spread(outgoing.reshape(peers, slots, width)).reshape(-1, width)
    flat = spread(ids).reshape(-1)

    def part_sum(part):
        onehot = (flat[None, :] == (part * mine + lax.iota(jnp.int32, mine))[:, None]).astype(f32)
        return jnp.dot(onehot, arrived, precision=high)

    parts = lax.map(part_sum, jnp.arange(pair)).reshape(pair * mine, width)
    total = lax.psum_scatter(parts, "tm", scatter_dimension=0, tiled=True)
    zero = jnp.zeros((mine, LANES), f32)
    return [zero] * 6 + [total]


def local(
    transactions,
    tx_product,
    tx_count,
    products,
    customers,
    send_rows,
    send_count,
    recv_customer,
    w_msg,
    w_prod_self,
    w_prod_agg,
    w_cust_self,
    w_cust_prod,
):
    peers, pair = lax.axis_size("hash"), lax.axis_size("tm")
    width = transactions.shape[1]
    mine = products.shape[0]
    send_slots = send_rows.shape[0] // peers
    place = jnp.stack([lax.axis_index("hash"), lax.axis_index("tm")]).astype(jnp.int32)

    if peers == 16 and pair == 2:
        parts = gathered_by_permutes(place, transactions, tx_product, tx_count, w_msg, mine)
    else:
        parts = gathered_plainly(transactions, tx_product, tx_count, w_msg, mine)

    product_self = jnp.dot(products, w_prod_self, precision=high)
    customer_self = jnp.dot(customers, w_cust_self, precision=high)
    send_index = lax.broadcasted_iota(jnp.int32, (peers, send_slots), 1)
    named = jnp.where(send_index < send_count[:, None], send_rows.reshape(peers, send_slots), -1)
    receivers = recv_customer.reshape(peers, send_slots)
    near = peers == 16 and pair == 2
    if near:
        order = (2, 3, 1, 0)
        named = by_distance(named, place, order).transpose(1, 0, 2)
        receivers = by_distance(receivers, place, order)
    picks = (named.reshape(-1)[:, None] == lax.iota(jnp.int32, mine)[None, :]).astype(bf16)
    incidence = (receivers.reshape(-1)[None, :] == lax.iota(jnp.int32, customers.shape[0])[:, None]).astype(bf16)

    counts = (4, 4, 2, 2, 2, 2) if near else (peers,)
    new_products, *listed = call(
        functools.partial(update_kernel, len(parts)),
        [products.shape] + [(n, send_slots, width) for n in counts],
        (*parts, product_self, products, *split_outside(w_prod_agg), picks),
    )
    if near:
        own, core, a2, b2, a3, b3 = listed
        incoming = deliver(own, core, a2, a3, b2, b3)
    else:
        incoming = [spread(listed[0])]
    (new_customers,) = call(
        final_kernel,
        [customers.shape],
        (incidence, customer_self, customers, *split_outside(w_cust_prod), *incoming),
    )
    return new_products, new_customers


def solution(mesh):
    rows, flat = P(("hash", "tm"), None), P(("hash", "tm"))
    placed = (rows, flat, flat, rows, rows, flat, flat, flat, P(), P(), P(), P(), P())
    return jax.shard_map(local, mesh=mesh, in_specs=placed, out_specs=(rows, rows), check_vma=False)
```

```python
import functools

import jax
import jax.numpy as jnp
from jax import lax
from jax.experimental import pallas as pl
from jax.experimental.pallas import tpu as pltpu
from jax.sharding import PartitionSpec as P

high = lax.Precision.HIGH
f32, bf16 = jnp.float32, jnp.bfloat16
LANES = 128
PAD = 8


def split(x):
    top = x.astype(bf16)
    return top, (x - top.astype(f32)).astype(bf16)


def split_outside(x):
    top = lax.reduce_precision(x, 8, 7)
    return top.astype(bf16), (x - top).astype(bf16)


def mm(a, b):
    return jnp.dot(a, b, preferred_element_type=f32)


def dot3(x, w_top, w_low):
    top, low = split(x)
    return mm(top, w_top) + (mm(low, w_top) + mm(top, w_low))


def dot2(picks, x):
    top, low = split(x)
    return mm(picks, top) + mm(picks, low)


def call(kernel, out, ins, smem=()):
    vmem = pl.BlockSpec(memory_space=pltpu.VMEM)
    scalar = pl.BlockSpec(memory_space=pltpu.SMEM)
    return pl.pallas_call(
        kernel,
        out_shape=[jax.ShapeDtypeStruct(s, f32) for s in out],
        in_specs=[scalar] * len(smem) + [vmem] * len(ins),
        out_specs=[vmem] * len(out),
        compiler_params=pltpu.CompilerParams(vmem_limit_bytes=32 * 1024 * 1024),
    )(*smem, *ins)


def lanes():
    return lax.broadcasted_iota(jnp.int32, (1, LANES), 1)


def message_kernel(place, count, tx, ids, w_top, w_low, own, core, l2, l3, r2, r3):
    near, far = place[0] & 3, place[0] >> 2
    slots = tx.shape[0] // 16
    lane = lanes()
    top, low = w_top[...], w_low[...]
    for m in (2, 3, 1, 0):
        c = near ^ m
        buckets = [4 * (far ^ k) + c for k in (2, 3, 1, 0)]
        x = jnp.concatenate([tx[pl.ds(pl.multiple_of(b * slots, slots), slots), :] for b in buckets], 0)
        y = jnp.maximum(dot3(x, top, low), 0.0)
        for i, b in enumerate(buckets):
            row = ids[pl.ds(b >> 1, 1), :]
            turned = pltpu.roll(row, slots, 1)
            twice = jnp.where((lane >= slots).astype(jnp.int32) == (c & 1), row, turned)
            twice = jnp.where((lane & (slots - 1)) < count[b], twice, -1).astype(f32)
            twice = jnp.broadcast_to(twice, (PAD, LANES))
            left, right = y[i * slots : (i + 1) * slots, :LANES], y[i * slots : (i + 1) * slots, LANES:]
            if m < 2:
                out = (own, core)[m]
                out[i, :slots, :] = left
                out[i, slots : 2 * slots, :] = right
                out[i, 2 * slots :, :] = twice
            elif i < 3:
                first, second = (l2, l3)[m - 2], (r2, r3)[m - 2]
                first[i, :slots, :] = left
                first[i, slots:, :] = twice
                second[i * slots : (i + 1) * slots, :] = right
            else:
                out = (r2, r3)[m - 2]
                out[3 * slots : 4 * slots, :] = left
                out[4 * slots : 5 * slots, :] = right
                out[5 * slots :, :] = twice


def targets(place, mine):
    row = lax.broadcasted_iota(jnp.int32, (2 * mine, LANES), 0)
    own = place[1]
    return jnp.where(row < mine, row + (1 - own) * mine, row - mine + own * mine).astype(f32)


def joined(one):
    lane = lanes()
    return [jnp.where(lane < LANES // 2, one[i], one[i + 1]) for i in (0, 2)]


def bucket_sum(rows, target, blocks, send, keep, at):
    mine = send.shape[1]
    picks = jnp.concatenate([(r == target).astype(bf16) for r in rows], 1)
    total = mm(picks, jnp.concatenate(split(jnp.concatenate(blocks, 0)), 1))
    total = total[:, :LANES] + total[:, LANES:]
    send[at] = total[:mine]
    keep[at] = total[mine:]


def left_kernel(place, own, core, l2, l3, send, keep, ids):
    target = targets(place, send.shape[1])
    senders = (own, core, l2, l3)
    slots = LANES // 2
    for z in range(3):
        rows = joined([block[z, pl.ds(block.shape[1] - PAD, 1), :] for block in senders])
        for i in range(2):
            ids[pl.ds(2 * z + i, 1), :] = rows[i]
        bucket_sum(rows, target, [block[z, :slots, :] for block in senders], send, keep, z)


def rest_kernel(place, ids, own, core, r2, r3, send, keep):
    target = targets(place, send.shape[1])
    slots = LANES // 2
    for z in range(3):
        rows = [ids[pl.ds(2 * z + i, 1), :] for i in range(2)]
        blocks = [block[z, slots : 2 * slots, :] for block in (own, core)]
        blocks += [block[z * slots : (z + 1) * slots, :] for block in (r2, r3)]
        bucket_sum(rows, target, blocks, send, keep, z)
    one = [block[3, pl.ds(2 * slots, 1), :] for block in (own, core)]
    rows = joined(one + [block[pl.ds(5 * slots, 1), :] for block in (r2, r3)])
    for side in range(2):
        blocks = [block[3, side * slots : (side + 1) * slots, :] for block in (own, core)]
        blocks += [block[(3 + side) * slots : (4 + side) * slots, :] for block in (r2, r3)]
        bucket_sum(rows, target, blocks, send, keep, 3 + side)


def pair_kernel(keep, got, *outs):
    for i in range(3):
        outs[i][...] = keep[i] + got[i]
    for own in outs[3:]:
        own[:, :LANES] = keep[3] + got[3]
        own[:, LANES:] = keep[4] + got[4]


def update_kernel(n, *refs):
    parts, (own, table, w_top, w_low, picks), (new, *outs) = refs[:n], refs[n : n + 5], refs[n + 5 :]
    wide = [part[...] for part in parts if part.shape[1] != LANES]
    left, right = (sum(part[...] for part in side) for side in (parts[:3], parts[3:6]))
    gathered = jnp.concatenate([left, right], 1) + sum(wide)
    fresh = table[...] + jnp.maximum(own[...] + dot3(gathered, w_top[...], w_low[...]), 0.0)
    new[...] = fresh
    listed = dot2(picks[...], fresh)
    at = 0
    for out in outs:
        rows = out.shape[0] * out.shape[1]
        out[...] = listed[at : at + rows].reshape(out.shape)
        at += rows


def turn_kernel(*refs):
    blocks, outs = refs[:4], refs[4:]
    for i, out in enumerate(outs):
        for m, block in enumerate(blocks):
            out[m] = block[i]


def final_kernel(incidence, own, table, w_top, w_low, *refs):
    incoming, new = refs[:-1], refs[-1]
    width = table.shape[1]
    rows = jnp.concatenate([block[...].reshape(-1, width) for block in incoming], 0)
    bought = dot2(incidence[...], rows)
    new[...] = table[...] + jnp.maximum(own[...] + dot3(bought, w_top[...], w_low[...]), 0.0)


def swap(x, axis, mask, size):
    return lax.ppermute(x, axis, [(i, i ^ mask) for i in range(size)])


def after(value, ready):
    return lax.optimization_barrier((*value, *ready))[: len(value)]


def spread(x):
    return lax.all_to_all(x, "hash", split_axis=0, concat_axis=0, tiled=True)


def gathered_by_permutes(place, transactions, tx_product, tx_count, w_msg, mine):
    peers = 16
    slots = transactions.shape[0] // peers
    own, core, l2, l3, r2, r3 = call(
        message_kernel,
        [(4, 2 * slots + PAD, LANES)] * 2 + [(3, slots + PAD, LANES)] * 2 + [(5 * slots + PAD, LANES)] * 2,
        (transactions, tx_product.reshape(-1, LANES), *split_outside(w_msg)),
        smem=(place, tx_count),
    )
    left, rest, part = (3, mine, LANES), (5, mine, LANES), (mine, LANES)

    def near(blocks):
        return [swap(block, "hash", mask, peers) for block, mask in zip(blocks, (2, 3))]

    def across(parts):
        return [swap(part, "hash", mask, peers) for part, mask in zip(parts, (8, 12, 4))]

    first = near((l2, l3))
    core = swap(core, "hash", 1, peers)
    second = near(after((r2, r3), first))
    send_l, keep_l, ids = call(left_kernel, [left, left, (8, LANES)], (own, core, *first), smem=(place,))
    got_l = swap(send_l, "tm", 1, 2)
    send_r, keep_r = call(rest_kernel, [rest, rest], (ids, own, core, *after(second, [got_l])), smem=(place,))
    got_r = swap(send_r, "tm", 1, 2)
    far_l = across(call(pair_kernel, [part] * 3, (keep_l, *after([got_l], [send_r]))))
    *parts_r, whole = call(pair_kernel, [part] * 3 + [(mine, 2 * LANES)], (keep_r, *after([got_r], far_l)))
    return [*far_l, *across(parts_r), whole]


def pick(x, i, axis):
    return lax.dynamic_index_in_dim(x, i, axis, keepdims=True)


def by_distance(x, place, zs):
    x = x.reshape(4, 4, -1)
    x = jnp.concatenate([pick(x, (place[0] >> 2) ^ k, 0) for k in zs], 0)
    return jnp.concatenate([pick(x, (place[0] & 3) ^ m, 1) for m in range(4)], 1)


def deliver(*blocks):
    peers = 16
    near = [blocks[0]] + [swap(blocks[m], "hash", m, peers) for m in (1, 2, 3)]
    two, three, one, own = call(turn_kernel, [blocks[0].shape] * 4, near)
    return [swap(two, "hash", 8, peers), swap(three, "hash", 12, peers), swap(one, "hash", 4, peers), own]


def gathered_plainly(transactions, tx_product, tx_count, w_msg, mine):
    peers, pair = lax.axis_size("hash"), lax.axis_size("tm")
    width = transactions.shape[1]
    slots = transactions.shape[0] // peers
    slot_index = lax.broadcasted_iota(jnp.int32, (peers, slots), 1)
    ids = jnp.where(slot_index < tx_count[:, None], tx_product.reshape(peers, slots), -1)
    outgoing = jax.nn.relu(jnp.dot(transactions, w_msg, precision=high))
    arrived = spread(outgoing.reshape(peers, slots, width)).reshape(-1, width)
    flat = spread(ids).reshape(-1)

    def part_sum(part):
        onehot = (flat[None, :] == (part * mine + lax.iota(jnp.int32, mine))[:, None]).astype(f32)
        return jnp.dot(onehot, arrived, precision=high)

    parts = lax.map(part_sum, jnp.arange(pair)).reshape(pair * mine, width)
    total = lax.psum_scatter(parts, "tm", scatter_dimension=0, tiled=True)
    zero = jnp.zeros((mine, LANES), f32)
    return [zero] * 6 + [total]


def local(
    transactions,
    tx_product,
    tx_count,
    products,
    customers,
    send_rows,
    send_count,
    recv_customer,
    w_msg,
    w_prod_self,
    w_prod_agg,
    w_cust_self,
    w_cust_prod,
):
    peers, pair = lax.axis_size("hash"), lax.axis_size("tm")
    width = transactions.shape[1]
    mine = products.shape[0]
    send_slots = send_rows.shape[0] // peers
    place = jnp.stack([lax.axis_index("hash"), lax.axis_index("tm")]).astype(jnp.int32)

    if peers == 16 and pair == 2:
        parts = gathered_by_permutes(place, transactions, tx_product, tx_count, w_msg, mine)
    else:
        parts = gathered_plainly(transactions, tx_product, tx_count, w_msg, mine)

    product_self = jnp.dot(products, w_prod_self, precision=high)
    customer_self = jnp.dot(customers, w_cust_self, precision=high)
    send_index = lax.broadcasted_iota(jnp.int32, (peers, send_slots), 1)
    named = jnp.where(send_index < send_count[:, None], send_rows.reshape(peers, send_slots), -1)
    receivers = recv_customer.reshape(peers, send_slots)
    near = peers == 16 and pair == 2
    if near:
        order = (2, 3, 1, 0)
        named = by_distance(named, place, order).transpose(1, 0, 2)
        receivers = by_distance(receivers, place, order)
    picks = (named.reshape(-1)[:, None] == lax.iota(jnp.int32, mine)[None, :]).astype(bf16)
    incidence = (receivers.reshape(-1)[None, :] == lax.iota(jnp.int32, customers.shape[0])[:, None]).astype(bf16)

    counts = (4, 4, 4, 4) if near else (peers,)
    new_products, *listed = call(
        functools.partial(update_kernel, len(parts)),
        [products.shape] + [(n, send_slots, width) for n in counts],
        (*parts, product_self, products, *split_outside(w_prod_agg), picks),
    )
    if near:
        incoming = deliver(*listed)
    else:
        incoming = [spread(listed[0])]
    (new_customers,) = call(
        final_kernel,
        [customers.shape],
        (incidence, customer_self, customers, *split_outside(w_cust_prod), *incoming),
    )
    return new_products, new_customers


def solution(mesh):
    rows, flat = P(("hash", "tm"), None), P(("hash", "tm"))
    placed = (rows, flat, flat, rows, rows, flat, flat, flat, P(), P(), P(), P(), P())
    return jax.shard_map(local, mesh=mesh, in_specs=placed, out_specs=(rows, rows), check_vma=False)
```

```python
import functools

import jax
import jax.numpy as jnp
from jax import lax
from jax.experimental import pallas as pl
from jax.experimental.pallas import tpu as pltpu
from jax.sharding import PartitionSpec as P

high = lax.Precision.HIGH
f32, bf16 = jnp.float32, jnp.bfloat16
LANES = 128
PAD = 8


def split(x):
    top = x.astype(bf16)
    return top, (x - top.astype(f32)).astype(bf16)


def split_outside(x):
    top = lax.reduce_precision(x, 8, 7)
    return top.astype(bf16), (x - top).astype(bf16)


def mm(a, b):
    return jnp.dot(a, b, preferred_element_type=f32)


def dot3(x, w_top, w_low):
    top, low = split(x)
    return mm(top, w_top) + (mm(low, w_top) + mm(top, w_low))


def dot2(picks, x):
    top, low = split(x)
    return mm(picks, top) + mm(picks, low)


def call(kernel, out, ins, smem=()):
    vmem = pl.BlockSpec(memory_space=pltpu.VMEM)
    scalar = pl.BlockSpec(memory_space=pltpu.SMEM)
    return pl.pallas_call(
        kernel,
        out_shape=[jax.ShapeDtypeStruct(s, f32) for s in out],
        in_specs=[scalar] * len(smem) + [vmem] * len(ins),
        out_specs=[vmem] * len(out),
        compiler_params=pltpu.CompilerParams(vmem_limit_bytes=32 * 1024 * 1024),
    )(*smem, *ins)


def lanes():
    return lax.broadcasted_iota(jnp.int32, (1, LANES), 1)


def message_kernel(place, count, tx, ids, w_top, w_low, own, core, l2, l3, r2, r3):
    near, far = place[0] & 3, place[0] >> 2
    slots = tx.shape[0] // 16
    lane = lanes()
    top, low = w_top[...], w_low[...]
    for m in (2, 3, 1, 0):
        c = near ^ m
        buckets = [4 * (far ^ k) + c for k in (2, 3, 1, 0)]
        x = jnp.concatenate([tx[pl.ds(pl.multiple_of(b * slots, slots), slots), :] for b in buckets], 0)
        y = jnp.maximum(dot3(x, top, low), 0.0)
        for i, b in enumerate(buckets):
            row = ids[pl.ds(b >> 1, 1), :]
            turned = pltpu.roll(row, slots, 1)
            twice = jnp.where((lane >= slots).astype(jnp.int32) == (c & 1), row, turned)
            twice = jnp.where((lane & (slots - 1)) < count[b], twice, -1).astype(f32)
            twice = jnp.broadcast_to(twice, (PAD, LANES))
            left, right = y[i * slots : (i + 1) * slots, :LANES], y[i * slots : (i + 1) * slots, LANES:]
            if m < 2:
                out = (own, core)[m]
                out[i, :slots, :] = left
                out[i, slots : 2 * slots, :] = right
                out[i, 2 * slots :, :] = twice
            elif i < 2:
                first, second = (l2, l3)[m - 2], (r2, r3)[m - 2]
                first[i, :slots, :] = left
                first[i, slots:, :] = twice
                second[i * slots : (i + 1) * slots, :] = right
            else:
                out, at = (r2, r3)[m - 2], 2 * slots + (i - 2) * (2 * slots + PAD)
                out[at : at + slots, :] = left
                out[at + slots : at + 2 * slots, :] = right
                out[at + 2 * slots : at + 2 * slots + PAD, :] = twice


def targets(place, mine):
    row = lax.broadcasted_iota(jnp.int32, (2 * mine, LANES), 0)
    own = place[1]
    return jnp.where(row < mine, row + (1 - own) * mine, row - mine + own * mine).astype(f32)


def joined(one):
    lane = lanes()
    return [jnp.where(lane < LANES // 2, one[i], one[i + 1]) for i in (0, 2)]


def bucket_sum(rows, target, blocks, send, keep, at):
    mine = send.shape[1]
    picks = jnp.concatenate([(r == target).astype(bf16) for r in rows], 1)
    total = mm(picks, jnp.concatenate(split(jnp.concatenate(blocks, 0)), 1))
    total = total[:, :LANES] + total[:, LANES:]
    send[at] = total[:mine]
    keep[at] = total[mine:]


def left_kernel(place, own, core, l2, l3, send, keep, ids):
    target = targets(place, send.shape[1])
    senders = (own, core, l2, l3)
    slots = LANES // 2
    for z in range(2):
        rows = joined([block[z, pl.ds(block.shape[1] - PAD, 1), :] for block in senders])
        for i in range(2):
            ids[pl.ds(2 * z + i, 1), :] = rows[i]
        bucket_sum(rows, target, [block[z, :slots, :] for block in senders], send, keep, z)


def rest_kernel(place, ids, own, core, r2, r3, send, keep):
    target = targets(place, send.shape[1])
    slots = LANES // 2
    for z in range(2):
        rows = [ids[pl.ds(2 * z + i, 1), :] for i in range(2)]
        blocks = [block[z, slots : 2 * slots, :] for block in (own, core)]
        blocks += [block[z * slots : (z + 1) * slots, :] for block in (r2, r3)]
        bucket_sum(rows, target, blocks, send, keep, z)
    for z in (2, 3):
        at = 2 * slots + (z - 2) * (2 * slots + PAD)
        one = [block[z, pl.ds(2 * slots, 1), :] for block in (own, core)]
        rows = joined(one + [block[pl.ds(at + 2 * slots, 1), :] for block in (r2, r3)])
        for side in range(2):
            blocks = [block[z, side * slots : (side + 1) * slots, :] for block in (own, core)]
            blocks += [block[at + side * slots : at + (side + 1) * slots, :] for block in (r2, r3)]
            bucket_sum(rows, target, blocks, send, keep, 2 * z - 2 + side)


def pair_kernel(keep, got, *outs):
    for i in range(2):
        outs[i][...] = keep[i] + got[i]
    for i, out in enumerate(outs[2:]):
        out[:, :LANES] = keep[2 * i + 2] + got[2 * i + 2]
        out[:, LANES:] = keep[2 * i + 3] + got[2 * i + 3]


def update_kernel(n, *refs):
    parts, (own, table, w_top, w_low, picks), (new, *outs) = refs[:n], refs[n : n + 5], refs[n + 5 :]
    wide = [part[...] for part in parts if part.shape[1] != LANES]
    left, right = (sum(part[...] for part in side) for side in (parts[:2], parts[2:4]))
    gathered = jnp.concatenate([left, right], 1) + sum(wide)
    fresh = table[...] + jnp.maximum(own[...] + dot3(gathered, w_top[...], w_low[...]), 0.0)
    new[...] = fresh
    listed = dot2(picks[...], fresh)
    at = 0
    for out in outs:
        rows = out.shape[0] * out.shape[1]
        out[...] = listed[at : at + rows].reshape(out.shape)
        at += rows


def turn_kernel(*refs):
    blocks, outs = refs[:4], refs[4:]
    for i, out in enumerate(outs):
        for m, block in enumerate(blocks):
            out[m] = block[i]


def final_kernel(incidence, own, table, w_top, w_low, *refs):
    incoming, new = refs[:-1], refs[-1]
    width = table.shape[1]
    rows = jnp.concatenate([block[...].reshape(-1, width) for block in incoming], 0)
    bought = dot2(incidence[...], rows)
    new[...] = table[...] + jnp.maximum(own[...] + dot3(bought, w_top[...], w_low[...]), 0.0)


def swap(x, axis, mask, size):
    return lax.ppermute(x, axis, [(i, i ^ mask) for i in range(size)])


def after(value, ready):
    return lax.optimization_barrier((*value, *ready))[: len(value)]


def spread(x):
    return lax.all_to_all(x, "hash", split_axis=0, concat_axis=0, tiled=True)


def gathered_by_permutes(place, transactions, tx_product, tx_count, w_msg, mine):
    peers = 16
    slots = transactions.shape[0] // peers
    own, core, l2, l3, r2, r3 = call(
        message_kernel,
        [(4, 2 * slots + PAD, LANES)] * 2 + [(2, slots + PAD, LANES)] * 2 + [(6 * slots + 2 * PAD, LANES)] * 2,
        (transactions, tx_product.reshape(-1, LANES), *split_outside(w_msg)),
        smem=(place, tx_count),
    )
    left, rest, part, wide = (2, mine, LANES), (6, mine, LANES), (mine, LANES), (mine, 2 * LANES)

    def near(blocks):
        return [swap(block, "hash", mask, peers) for block, mask in zip(blocks, (2, 3))]

    def across(parts):
        return [swap(part, "hash", mask, peers) for part, mask in zip(parts, (8, 12))]

    first = near((l2, l3))
    core = swap(core, "hash", 1, peers)
    second = near((r2, r3))
    send_l, keep_l, ids = call(left_kernel, [left, left, (8, LANES)], (own, core, *first), smem=(place,))
    got_l = swap(send_l, "tm", 1, 2)
    send_r, keep_r = call(rest_kernel, [rest, rest], (ids, own, core, *after(second, [got_l])), smem=(place,))
    got_r = swap(send_r, "tm", 1, 2)
    far_l = across(call(pair_kernel, [part] * 2, (keep_l, *after([got_l], [send_r]))))
    *parts_r, next_to, whole = call(pair_kernel, [part] * 2 + [wide] * 2, (keep_r, *after([got_r], far_l)))
    return [*far_l, *across(parts_r), swap(next_to, "hash", 4, peers), whole]


def pick(x, i, axis):
    return lax.dynamic_index_in_dim(x, i, axis, keepdims=True)


def by_distance(x, place, zs):
    x = x.reshape(4, 4, -1)
    x = jnp.concatenate([pick(x, (place[0] >> 2) ^ k, 0) for k in zs], 0)
    return jnp.concatenate([pick(x, (place[0] & 3) ^ m, 1) for m in range(4)], 1)


def deliver(*blocks):
    peers = 16
    near = [blocks[0]] + [swap(blocks[m], "hash", m, peers) for m in (1, 2, 3)]
    two, three, one, own = call(turn_kernel, [blocks[0].shape] * 4, near)
    return [swap(two, "hash", 8, peers), swap(three, "hash", 12, peers), swap(one, "hash", 4, peers), own]


def gathered_plainly(transactions, tx_product, tx_count, w_msg, mine):
    peers, pair = lax.axis_size("hash"), lax.axis_size("tm")
    width = transactions.shape[1]
    slots = transactions.shape[0] // peers
    slot_index = lax.broadcasted_iota(jnp.int32, (peers, slots), 1)
    ids = jnp.where(slot_index < tx_count[:, None], tx_product.reshape(peers, slots), -1)
    outgoing = jax.nn.relu(jnp.dot(transactions, w_msg, precision=high))
    arrived = spread(outgoing.reshape(peers, slots, width)).reshape(-1, width)
    flat = spread(ids).reshape(-1)

    def part_sum(part):
        onehot = (flat[None, :] == (part * mine + lax.iota(jnp.int32, mine))[:, None]).astype(f32)
        return jnp.dot(onehot, arrived, precision=high)

    parts = lax.map(part_sum, jnp.arange(pair)).reshape(pair * mine, width)
    total = lax.psum_scatter(parts, "tm", scatter_dimension=0, tiled=True)
    zero = jnp.zeros((mine, LANES), f32)
    return [zero] * 4 + [total]


def local(
    transactions,
    tx_product,
    tx_count,
    products,
    customers,
    send_rows,
    send_count,
    recv_customer,
    w_msg,
    w_prod_self,
    w_prod_agg,
    w_cust_self,
    w_cust_prod,
):
    peers, pair = lax.axis_size("hash"), lax.axis_size("tm")
    width = transactions.shape[1]
    mine = products.shape[0]
    send_slots = send_rows.shape[0] // peers
    place = jnp.stack([lax.axis_index("hash"), lax.axis_index("tm")]).astype(jnp.int32)

    if peers == 16 and pair == 2:
        parts = gathered_by_permutes(place, transactions, tx_product, tx_count, w_msg, mine)
    else:
        parts = gathered_plainly(transactions, tx_product, tx_count, w_msg, mine)

    product_self = jnp.dot(products, w_prod_self, precision=high)
    customer_self = jnp.dot(customers, w_cust_self, precision=high)
    send_index = lax.broadcasted_iota(jnp.int32, (peers, send_slots), 1)
    named = jnp.where(send_index < send_count[:, None], send_rows.reshape(peers, send_slots), -1)
    receivers = recv_customer.reshape(peers, send_slots)
    near = peers == 16 and pair == 2
    if near:
        order = (2, 3, 1, 0)
        named = by_distance(named, place, order).transpose(1, 0, 2)
        receivers = by_distance(receivers, place, order)
    picks = (named.reshape(-1)[:, None] == lax.iota(jnp.int32, mine)[None, :]).astype(bf16)
    incidence = (receivers.reshape(-1)[None, :] == lax.iota(jnp.int32, customers.shape[0])[:, None]).astype(bf16)

    counts = (4, 4, 4, 4) if near else (peers,)
    new_products, *listed = call(
        functools.partial(update_kernel, len(parts)),
        [products.shape] + [(n, send_slots, width) for n in counts],
        (*parts, product_self, products, *split_outside(w_prod_agg), picks),
    )
    if near:
        incoming = deliver(*listed)
    else:
        incoming = [spread(listed[0])]
    (new_customers,) = call(
        final_kernel,
        [customers.shape],
        (incidence, customer_self, customers, *split_outside(w_cust_prod), *incoming),
    )
    return new_products, new_customers


def solution(mesh):
    rows, flat = P(("hash", "tm"), None), P(("hash", "tm"))
    placed = (rows, flat, flat, rows, rows, flat, flat, flat, P(), P(), P(), P(), P())
    return jax.shard_map(local, mesh=mesh, in_specs=placed, out_specs=(rows, rows), check_vma=False)
```

```python
import functools

import jax
import jax.numpy as jnp
from jax import lax
from jax.experimental import pallas as pl
from jax.experimental.pallas import tpu as pltpu
from jax.sharding import PartitionSpec as P

high = lax.Precision.HIGH
f32, bf16 = jnp.float32, jnp.bfloat16
LANES = 128
PAD = 8


def split(x):
    top = x.astype(bf16)
    return top, (x - top.astype(f32)).astype(bf16)


def split_outside(x):
    top = lax.reduce_precision(x, 8, 7)
    return top.astype(bf16), (x - top).astype(bf16)


def mm(a, b):
    return jnp.dot(a, b, preferred_element_type=f32)


def dot3(x, w_top, w_low):
    top, low = split(x)
    return mm(top, w_top) + (mm(low, w_top) + mm(top, w_low))


def dot2(picks, x):
    top, low = split(x)
    return mm(picks, top) + mm(picks, low)


def call(kernel, out, ins, smem=()):
    vmem = pl.BlockSpec(memory_space=pltpu.VMEM)
    scalar = pl.BlockSpec(memory_space=pltpu.SMEM)
    return pl.pallas_call(
        kernel,
        out_shape=[jax.ShapeDtypeStruct(s, f32) for s in out],
        in_specs=[scalar] * len(smem) + [vmem] * len(ins),
        out_specs=[vmem] * len(out),
        compiler_params=pltpu.CompilerParams(vmem_limit_bytes=32 * 1024 * 1024),
    )(*smem, *ins)


def lanes():
    return lax.broadcasted_iota(jnp.int32, (1, LANES), 1)


def message_kernel(place, count, tx, ids, w_top, w_low, own, core, l2, l3, r2, r3):
    near, far = place[0] & 3, place[0] >> 2
    slots = tx.shape[0] // 16
    lane = lanes()
    top, low = w_top[...], w_low[...]
    for m in (2, 3, 1, 0):
        c = near ^ m
        buckets = [4 * (far ^ k) + c for k in (2, 3, 1, 0)]
        x = jnp.concatenate([tx[pl.ds(pl.multiple_of(b * slots, slots), slots), :] for b in buckets], 0)
        y = jnp.maximum(dot3(x, top, low), 0.0)
        for i, b in enumerate(buckets):
            row = ids[pl.ds(b >> 1, 1), :]
            turned = pltpu.roll(row, slots, 1)
            twice = jnp.where((lane >= slots).astype(jnp.int32) == (c & 1), row, turned)
            twice = jnp.where((lane & (slots - 1)) < count[b], twice, -1).astype(f32)
            twice = jnp.broadcast_to(twice, (PAD, LANES))
            left, right = y[i * slots : (i + 1) * slots, :LANES], y[i * slots : (i + 1) * slots, LANES:]
            if m < 2:
                out = (own, core)[m]
                out[i, :slots, :] = left
                out[i, slots : 2 * slots, :] = right
                out[i, 2 * slots :, :] = twice
            elif i < 2:
                first, second = (l2, l3)[m - 2], (r2, r3)[m - 2]
                first[i, :slots, :] = left
                first[i, slots:, :] = twice
                second[i * slots : (i + 1) * slots, :] = right
            else:
                out, at = (r2, r3)[m - 2], 2 * slots + (i - 2) * (2 * slots + PAD)
                out[at : at + slots, :] = left
                out[at + slots : at + 2 * slots, :] = right
                out[at + 2 * slots : at + 2 * slots + PAD, :] = twice


def targets(place, mine):
    row = lax.broadcasted_iota(jnp.int32, (2 * mine, LANES), 0)
    own = place[1]
    return jnp.where(row < mine, row + (1 - own) * mine, row - mine + own * mine).astype(f32)


def joined(one):
    lane = lanes()
    return [jnp.where(lane < LANES // 2, one[i], one[i + 1]) for i in (0, 2)]


def bucket_sum(rows, target, blocks, send, keep, at):
    mine = send.shape[1]
    picks = jnp.concatenate([(r == target).astype(bf16) for r in rows], 1)
    total = mm(picks, jnp.concatenate(split(jnp.concatenate(blocks, 0)), 1))
    total = total[:, :LANES] + total[:, LANES:]
    send[at] = total[:mine]
    keep[at] = total[mine:]


def left_kernel(place, own, core, l2, l3, send, keep, ids):
    target = targets(place, send.shape[1])
    senders = (own, core, l2, l3)
    slots = LANES // 2
    for z in range(2):
        rows = joined([block[z, pl.ds(block.shape[1] - PAD, 1), :] for block in senders])
        for i in range(2):
            ids[pl.ds(2 * z + i, 1), :] = rows[i]
        bucket_sum(rows, target, [block[z, :slots, :] for block in senders], send, keep, z)


def rest_kernel(place, ids, own, core, r2, r3, send, keep):
    target = targets(place, send.shape[1])
    slots = LANES // 2
    for z in range(2):
        rows = [ids[pl.ds(2 * z + i, 1), :] for i in range(2)]
        blocks = [block[z, slots : 2 * slots, :] for block in (own, core)]
        blocks += [block[z * slots : (z + 1) * slots, :] for block in (r2, r3)]
        bucket_sum(rows, target, blocks, send, keep, z)
    for z in (2, 3):
        at = 2 * slots + (z - 2) * (2 * slots + PAD)
        one = [block[z, pl.ds(2 * slots, 1), :] for block in (own, core)]
        rows = joined(one + [block[pl.ds(at + 2 * slots, 1), :] for block in (r2, r3)])
        for side in range(2):
            blocks = [block[z, side * slots : (side + 1) * slots, :] for block in (own, core)]
            blocks += [block[at + side * slots : at + (side + 1) * slots, :] for block in (r2, r3)]
            bucket_sum(rows, target, blocks, send, keep, 2 * z - 2 + side)


def pair_kernel(keep, got, *outs):
    for i, out in enumerate(outs[:4]):
        out[...] = keep[i] + got[i]
    for own in outs[4:]:
        own[:, :LANES] = keep[4] + got[4]
        own[:, LANES:] = keep[5] + got[5]


def update_kernel(n, *refs):
    parts, (own, table, w_top, w_low, picks), (new, *outs) = refs[:n], refs[n : n + 5], refs[n + 5 :]
    wide = [part[...] for part in parts if part.shape[1] != LANES]
    left, right = (sum(part[...] for part in side) for side in ((*parts[:2], parts[4]), (*parts[2:4], parts[5])))
    gathered = jnp.concatenate([left, right], 1) + sum(wide)
    fresh = table[...] + jnp.maximum(own[...] + dot3(gathered, w_top[...], w_low[...]), 0.0)
    new[...] = fresh
    listed = dot2(picks[...], fresh)
    at = 0
    for out in outs:
        rows = out.shape[0] * out.shape[1]
        out[...] = listed[at : at + rows].reshape(out.shape)
        at += rows


def turn_kernel(*refs):
    blocks, outs = refs[:4], refs[4:]
    for i, out in enumerate(outs):
        for m, block in enumerate(blocks):
            out[m] = block[i]


def final_kernel(incidence, own, table, w_top, w_low, *refs):
    incoming, new = refs[:-1], refs[-1]
    width = table.shape[1]
    rows = jnp.concatenate([block[...].reshape(-1, width) for block in incoming], 0)
    bought = dot2(incidence[...], rows)
    new[...] = table[...] + jnp.maximum(own[...] + dot3(bought, w_top[...], w_low[...]), 0.0)


def swap(x, axis, mask, size):
    return lax.ppermute(x, axis, [(i, i ^ mask) for i in range(size)])


def after(value, ready):
    return lax.optimization_barrier((*value, *ready))[: len(value)]


def spread(x):
    return lax.all_to_all(x, "hash", split_axis=0, concat_axis=0, tiled=True)


def gathered_by_permutes(place, transactions, tx_product, tx_count, w_msg, mine):
    peers = 16
    slots = transactions.shape[0] // peers
    own, core, l2, l3, r2, r3 = call(
        message_kernel,
        [(4, 2 * slots + PAD, LANES)] * 2 + [(2, slots + PAD, LANES)] * 2 + [(6 * slots + 2 * PAD, LANES)] * 2,
        (transactions, tx_product.reshape(-1, LANES), *split_outside(w_msg)),
        smem=(place, tx_count),
    )
    left, rest, part, wide = (2, mine, LANES), (6, mine, LANES), (mine, LANES), (mine, 2 * LANES)

    def near(blocks):
        return [swap(block, "hash", mask, peers) for block, mask in zip(blocks, (2, 3))]

    def across(parts):
        return [swap(part, "hash", mask, peers) for part, mask in zip(parts, (8, 12))]

    first = near((l2, l3))
    core = swap(core, "hash", 1, peers)
    second = near((r2, r3))
    send_l, keep_l, ids = call(left_kernel, [left, left, (8, LANES)], (own, core, *first), smem=(place,))
    got_l = swap(send_l, "tm", 1, 2)
    send_r, keep_r = call(rest_kernel, [rest, rest], (ids, own, core, *after(second, [got_l])), smem=(place,))
    got_r = swap(send_r, "tm", 1, 2)
    far_l = across(call(pair_kernel, [part] * 2, (keep_l, *after([got_l], [send_r]))))
    *parts_r, near_l, near_r, whole = call(pair_kernel, [part] * 4 + [wide], (keep_r, *after([got_r], far_l)))
    far_r = across(parts_r)
    return [*far_l, *far_r, swap(near_l, "hash", 4, peers), swap(near_r, "hash", 4, peers), whole]


def pick(x, i, axis):
    return lax.dynamic_index_in_dim(x, i, axis, keepdims=True)


def by_distance(x, place, zs):
    x = x.reshape(4, 4, -1)
    x = jnp.concatenate([pick(x, (place[0] >> 2) ^ k, 0) for k in zs], 0)
    return jnp.concatenate([pick(x, (place[0] & 3) ^ m, 1) for m in range(4)], 1)


def deliver(*blocks):
    peers = 16
    near = [blocks[0]] + [swap(blocks[m], "hash", m, peers) for m in (1, 2, 3)]
    two, three, one, own = call(turn_kernel, [blocks[0].shape] * 4, near)
    return [swap(two, "hash", 8, peers), swap(three, "hash", 12, peers), swap(one, "hash", 4, peers), own]


def gathered_plainly(transactions, tx_product, tx_count, w_msg, mine):
    peers, pair = lax.axis_size("hash"), lax.axis_size("tm")
    width = transactions.shape[1]
    slots = transactions.shape[0] // peers
    slot_index = lax.broadcasted_iota(jnp.int32, (peers, slots), 1)
    ids = jnp.where(slot_index < tx_count[:, None], tx_product.reshape(peers, slots), -1)
    outgoing = jax.nn.relu(jnp.dot(transactions, w_msg, precision=high))
    arrived = spread(outgoing.reshape(peers, slots, width)).reshape(-1, width)
    flat = spread(ids).reshape(-1)

    def part_sum(part):
        onehot = (flat[None, :] == (part * mine + lax.iota(jnp.int32, mine))[:, None]).astype(f32)
        return jnp.dot(onehot, arrived, precision=high)

    parts = lax.map(part_sum, jnp.arange(pair)).reshape(pair * mine, width)
    total = lax.psum_scatter(parts, "tm", scatter_dimension=0, tiled=True)
    zero = jnp.zeros((mine, LANES), f32)
    return [zero] * 6 + [total]


def local(
    transactions,
    tx_product,
    tx_count,
    products,
    customers,
    send_rows,
    send_count,
    recv_customer,
    w_msg,
    w_prod_self,
    w_prod_agg,
    w_cust_self,
    w_cust_prod,
):
    peers, pair = lax.axis_size("hash"), lax.axis_size("tm")
    width = transactions.shape[1]
    mine = products.shape[0]
    send_slots = send_rows.shape[0] // peers
    place = jnp.stack([lax.axis_index("hash"), lax.axis_index("tm")]).astype(jnp.int32)

    if peers == 16 and pair == 2:
        parts = gathered_by_permutes(place, transactions, tx_product, tx_count, w_msg, mine)
    else:
        parts = gathered_plainly(transactions, tx_product, tx_count, w_msg, mine)

    product_self = jnp.dot(products, w_prod_self, precision=high)
    customer_self = jnp.dot(customers, w_cust_self, precision=high)
    send_index = lax.broadcasted_iota(jnp.int32, (peers, send_slots), 1)
    named = jnp.where(send_index < send_count[:, None], send_rows.reshape(peers, send_slots), -1)
    receivers = recv_customer.reshape(peers, send_slots)
    near = peers == 16 and pair == 2
    if near:
        order = (2, 3, 1, 0)
        named = by_distance(named, place, order).transpose(1, 0, 2)
        receivers = by_distance(receivers, place, order)
    picks = (named.reshape(-1)[:, None] == lax.iota(jnp.int32, mine)[None, :]).astype(bf16)
    incidence = (receivers.reshape(-1)[None, :] == lax.iota(jnp.int32, customers.shape[0])[:, None]).astype(bf16)

    counts = (4, 4, 4, 4) if near else (peers,)
    new_products, *listed = call(
        functools.partial(update_kernel, len(parts)),
        [products.shape] + [(n, send_slots, width) for n in counts],
        (*parts, product_self, products, *split_outside(w_prod_agg), picks),
    )
    if near:
        incoming = deliver(*listed)
    else:
        incoming = [spread(listed[0])]
    (new_customers,) = call(
        final_kernel,
        [customers.shape],
        (incidence, customer_self, customers, *split_outside(w_cust_prod), *incoming),
    )
    return new_products, new_customers


def solution(mesh):
    rows, flat = P(("hash", "tm"), None), P(("hash", "tm"))
    placed = (rows, flat, flat, rows, rows, flat, flat, flat, P(), P(), P(), P(), P())
    return jax.shard_map(local, mesh=mesh, in_specs=placed, out_specs=(rows, rows), check_vma=False)
```

```python
import functools

import jax
import jax.numpy as jnp
from jax import lax
from jax.experimental import pallas as pl
from jax.experimental.pallas import tpu as pltpu
from jax.sharding import PartitionSpec as P

high = lax.Precision.HIGH
f32, bf16 = jnp.float32, jnp.bfloat16
LANES = 128
PAD = 8


def split(x):
    top = x.astype(bf16)
    return top, (x - top.astype(f32)).astype(bf16)


def split_outside(x):
    top = lax.reduce_precision(x, 8, 7)
    return top.astype(bf16), (x - top).astype(bf16)


def mm(a, b):
    return jnp.dot(a, b, preferred_element_type=f32)


def dot3(x, w_top, w_low):
    top, low = split(x)
    return mm(top, w_top) + (mm(low, w_top) + mm(top, w_low))


def dot2(picks, x):
    top, low = split(x)
    return mm(picks, top) + mm(picks, low)


def call(kernel, out, ins, smem=()):
    vmem = pl.BlockSpec(memory_space=pltpu.VMEM)
    scalar = pl.BlockSpec(memory_space=pltpu.SMEM)
    return pl.pallas_call(
        kernel,
        out_shape=[jax.ShapeDtypeStruct(s, f32) for s in out],
        in_specs=[scalar] * len(smem) + [vmem] * len(ins),
        out_specs=[vmem] * len(out),
        compiler_params=pltpu.CompilerParams(vmem_limit_bytes=32 * 1024 * 1024),
    )(*smem, *ins)


def lanes():
    return lax.broadcasted_iota(jnp.int32, (1, LANES), 1)


def message_kernel(place, count, tx, ids, w_top, w_low, own, core, l2, l3, r2, r3):
    near, far = place[0] & 3, place[0] >> 2
    slots = tx.shape[0] // 16
    lane = lanes()
    top, low = w_top[...], w_low[...]
    for m in (2, 3, 1, 0):
        c = near ^ m
        buckets = [4 * (far ^ k) + c for k in (2, 3, 1, 0)]
        x = jnp.concatenate([tx[pl.ds(pl.multiple_of(b * slots, slots), slots), :] for b in buckets], 0)
        y = jnp.maximum(dot3(x, top, low), 0.0)
        for i, b in enumerate(buckets):
            row = ids[pl.ds(b >> 1, 1), :]
            turned = pltpu.roll(row, slots, 1)
            twice = jnp.where((lane >= slots).astype(jnp.int32) == (c & 1), row, turned)
            twice = jnp.where((lane & (slots - 1)) < count[b], twice, -1).astype(f32)
            left, right = y[i * slots : (i + 1) * slots, :LANES], y[i * slots : (i + 1) * slots, LANES:]
            if m < 2:
                out = (own, core)[m]
                out[i, :slots, :] = left
                out[i, slots : 2 * slots, :] = right
                out[i, 2 * slots :, :] = jnp.broadcast_to(twice, (PAD, LANES))
                continue
            first, second = (l2, l3)[m - 2], (r2, r3)[m - 2]
            if i == 0:
                first[2 * slots :, :] = jnp.broadcast_to(twice, (PAD, LANES))
            first[2 * slots + i : 2 * slots + i + 1, :] = twice
            if i < 2:
                first[i * slots : (i + 1) * slots, :] = left
                second[i * slots : (i + 1) * slots, :] = right
            else:
                at = 2 * (i - 1) * slots
                second[at : at + slots, :] = left
                second[at + slots : at + 2 * slots, :] = right


def targets(place, mine):
    row = lax.broadcasted_iota(jnp.int32, (2 * mine, LANES), 0)
    own = place[1]
    return jnp.where(row < mine, row + (1 - own) * mine, row - mine + own * mine).astype(f32)


def joined(one):
    lane = lanes()
    return [jnp.where(lane < LANES // 2, one[i], one[i + 1]) for i in (0, 2)]


def bucket_sum(rows, target, blocks, send, keep, at):
    mine = send.shape[1]
    picks = jnp.concatenate([(r == target).astype(bf16) for r in rows], 1)
    total = mm(picks, jnp.concatenate(split(jnp.concatenate(blocks, 0)), 1))
    total = total[:, :LANES] + total[:, LANES:]
    send[at] = total[:mine]
    keep[at] = total[mine:]


def left_kernel(place, own, core, l2, l3, send, keep, ids):
    target = targets(place, send.shape[1])
    slots = LANES // 2
    for z in range(4):
        one = [block[z, pl.ds(2 * slots, 1), :] for block in (own, core)]
        rows = joined(one + [block[pl.ds(2 * slots + z, 1), :] for block in (l2, l3)])
        for i in range(2):
            ids[pl.ds(2 * z + i, 1), :] = rows[i]
        if z < 2:
            blocks = [block[z, :slots, :] for block in (own, core)]
            blocks += [block[z * slots : (z + 1) * slots, :] for block in (l2, l3)]
            bucket_sum(rows, target, blocks, send, keep, z)


def rest_kernel(place, ids, own, core, r2, r3, send, keep):
    target = targets(place, send.shape[1])
    slots = LANES // 2
    jobs = [(0, 1), (1, 1), (2, 0), (2, 1), (3, 0), (3, 1)]
    for at, (z, side) in enumerate(jobs):
        rows = [ids[pl.ds(2 * z + i, 1), :] for i in range(2)]
        blocks = [block[z, side * slots : (side + 1) * slots, :] for block in (own, core)]
        blocks += [block[at * slots : (at + 1) * slots, :] for block in (r2, r3)]
        bucket_sum(rows, target, blocks, send, keep, at)


def pair_kernel(keep, got, *outs):
    for i, out in enumerate(outs[:4]):
        out[...] = keep[i] + got[i]
    for own in outs[4:]:
        own[:, :LANES] = keep[4] + got[4]
        own[:, LANES:] = keep[5] + got[5]


def update_kernel(n, *refs):
    parts, (own, table, w_top, w_low, picks), (new, *outs) = refs[:n], refs[n : n + 5], refs[n + 5 :]
    wide = [part[...] for part in parts if part.shape[1] != LANES]
    left, right = (sum(part[...] for part in side) for side in ((*parts[:2], parts[4]), (*parts[2:4], parts[5])))
    gathered = jnp.concatenate([left, right], 1) + sum(wide)
    fresh = table[...] + jnp.maximum(own[...] + dot3(gathered, w_top[...], w_low[...]), 0.0)
    new[...] = fresh
    listed = dot2(picks[...], fresh)
    at = 0
    for out in outs:
        rows = out.shape[0] * out.shape[1]
        out[...] = listed[at : at + rows].reshape(out.shape)
        at += rows


def turn_kernel(*refs):
    blocks, outs = refs[:4], refs[4:]
    for i, out in enumerate(outs):
        for m, block in enumerate(blocks):
            out[m] = block[i]


def final_kernel(incidence, own, table, w_top, w_low, *refs):
    incoming, new = refs[:-1], refs[-1]
    width = table.shape[1]
    rows = jnp.concatenate([block[...].reshape(-1, width) for block in incoming], 0)
    bought = dot2(incidence[...], rows)
    new[...] = table[...] + jnp.maximum(own[...] + dot3(bought, w_top[...], w_low[...]), 0.0)


def swap(x, axis, mask, size):
    return lax.ppermute(x, axis, [(i, i ^ mask) for i in range(size)])


def after(value, ready):
    return lax.optimization_barrier((*value, *ready))[: len(value)]


def spread(x):
    return lax.all_to_all(x, "hash", split_axis=0, concat_axis=0, tiled=True)


def gathered_by_permutes(place, transactions, tx_product, tx_count, w_msg, mine):
    peers = 16
    slots = transactions.shape[0] // peers
    own, core, l2, l3, r2, r3 = call(
        message_kernel,
        [(4, 2 * slots + PAD, LANES)] * 2 + [(2 * slots + PAD, LANES)] * 2 + [(6 * slots, LANES)] * 2,
        (transactions, tx_product.reshape(-1, LANES), *split_outside(w_msg)),
        smem=(place, tx_count),
    )
    left, rest, part, wide = (2, mine, LANES), (6, mine, LANES), (mine, LANES), (mine, 2 * LANES)

    def near(blocks):
        return [swap(block, "hash", mask, peers) for block, mask in zip(blocks, (2, 3))]

    def across(parts):
        return [swap(part, "hash", mask, peers) for part, mask in zip(parts, (8, 12))]

    first = near((l2, l3))
    core = swap(core, "hash", 1, peers)
    second = near((r2, r3))
    send_l, keep_l, ids = call(left_kernel, [left, left, (8, LANES)], (own, core, *first), smem=(place,))
    got_l = swap(send_l, "tm", 1, 2)
    send_r, keep_r = call(rest_kernel, [rest, rest], (ids, own, core, *after(second, [got_l])), smem=(place,))
    got_r = swap(send_r, "tm", 1, 2)
    far_l = across(call(pair_kernel, [part] * 2, (keep_l, *after([got_l], [send_r]))))
    *parts_r, near_l, near_r, whole = call(pair_kernel, [part] * 4 + [wide], (keep_r, *after([got_r], far_l)))
    far_r = across(parts_r)
    return [*far_l, *far_r, swap(near_l, "hash", 4, peers), swap(near_r, "hash", 4, peers), whole]


def pick(x, i, axis):
    return lax.dynamic_index_in_dim(x, i, axis, keepdims=True)


def by_distance(x, place, zs):
    x = x.reshape(4, 4, -1)
    x = jnp.concatenate([pick(x, (place[0] >> 2) ^ k, 0) for k in zs], 0)
    return jnp.concatenate([pick(x, (place[0] & 3) ^ m, 1) for m in range(4)], 1)


def deliver(*blocks):
    peers = 16
    near = [blocks[0]] + [swap(blocks[m], "hash", m, peers) for m in (1, 2, 3)]
    two, three, one, own = call(turn_kernel, [blocks[0].shape] * 4, near)
    return [swap(two, "hash", 8, peers), swap(three, "hash", 12, peers), swap(one, "hash", 4, peers), own]


def gathered_plainly(transactions, tx_product, tx_count, w_msg, mine):
    peers, pair = lax.axis_size("hash"), lax.axis_size("tm")
    width = transactions.shape[1]
    slots = transactions.shape[0] // peers
    slot_index = lax.broadcasted_iota(jnp.int32, (peers, slots), 1)
    ids = jnp.where(slot_index < tx_count[:, None], tx_product.reshape(peers, slots), -1)
    outgoing = jax.nn.relu(jnp.dot(transactions, w_msg, precision=high))
    arrived = spread(outgoing.reshape(peers, slots, width)).reshape(-1, width)
    flat = spread(ids).reshape(-1)

    def part_sum(part):
        onehot = (flat[None, :] == (part * mine + lax.iota(jnp.int32, mine))[:, None]).astype(f32)
        return jnp.dot(onehot, arrived, precision=high)

    parts = lax.map(part_sum, jnp.arange(pair)).reshape(pair * mine, width)
    total = lax.psum_scatter(parts, "tm", scatter_dimension=0, tiled=True)
    zero = jnp.zeros((mine, LANES), f32)
    return [zero] * 6 + [total]


def local(
    transactions,
    tx_product,
    tx_count,
    products,
    customers,
    send_rows,
    send_count,
    recv_customer,
    w_msg,
    w_prod_self,
    w_prod_agg,
    w_cust_self,
    w_cust_prod,
):
    peers, pair = lax.axis_size("hash"), lax.axis_size("tm")
    width = transactions.shape[1]
    mine = products.shape[0]
    send_slots = send_rows.shape[0] // peers
    place = jnp.stack([lax.axis_index("hash"), lax.axis_index("tm")]).astype(jnp.int32)

    if peers == 16 and pair == 2:
        parts = gathered_by_permutes(place, transactions, tx_product, tx_count, w_msg, mine)
    else:
        parts = gathered_plainly(transactions, tx_product, tx_count, w_msg, mine)

    product_self = jnp.dot(products, w_prod_self, precision=high)
    customer_self = jnp.dot(customers, w_cust_self, precision=high)
    send_index = lax.broadcasted_iota(jnp.int32, (peers, send_slots), 1)
    named = jnp.where(send_index < send_count[:, None], send_rows.reshape(peers, send_slots), -1)
    receivers = recv_customer.reshape(peers, send_slots)
    near = peers == 16 and pair == 2
    if near:
        order = (2, 3, 1, 0)
        named = by_distance(named, place, order).transpose(1, 0, 2)
        receivers = by_distance(receivers, place, order)
    picks = (named.reshape(-1)[:, None] == lax.iota(jnp.int32, mine)[None, :]).astype(bf16)
    incidence = (receivers.reshape(-1)[None, :] == lax.iota(jnp.int32, customers.shape[0])[:, None]).astype(bf16)

    counts = (4, 4, 4, 4) if near else (peers,)
    new_products, *listed = call(
        functools.partial(update_kernel, len(parts)),
        [products.shape] + [(n, send_slots, width) for n in counts],
        (*parts, product_self, products, *split_outside(w_prod_agg), picks),
    )
    if near:
        incoming = deliver(*listed)
    else:
        incoming = [spread(listed[0])]
    (new_customers,) = call(
        final_kernel,
        [customers.shape],
        (incidence, customer_self, customers, *split_outside(w_cust_prod), *incoming),
    )
    return new_products, new_customers


def solution(mesh):
    rows, flat = P(("hash", "tm"), None), P(("hash", "tm"))
    placed = (rows, flat, flat, rows, rows, flat, flat, flat, P(), P(), P(), P(), P())
    return jax.shard_map(local, mesh=mesh, in_specs=placed, out_specs=(rows, rows), check_vma=False)
```
